128 devices in a mesh: dp: 2 (over z_hi), expert: 8 (over y, core), tensor: 8 (over z_lo, x).
Axes of the slice: x: 4, y: 4, z: 4 (z_hi: 2, z_lo: 2; z = z_hi * 2 + z_lo), core: 2. Of those that a mesh axis runs over, the one named last changes fastest.
Arguments:
- tokens: bfloat16 [2048, 3072], P(('dp', 'expert')), may hold values from -6 to 6
- cotangent: bfloat16 [2048, 3072], P(('dp', 'expert', 'tensor')), may hold values from -6 to 6
- expert_ids: int32 [2048, 2], P(('dp', 'expert')), may hold values from 0 to 7, all different within a row; in each aligned block of 128 rows (0 to 127, 128 to 255, ...) at most 36 rows name the same one
- route_weight: float32 [2048, 2], P(('dp', 'expert')), may hold values from 0.1 to 1
- w_up: bfloat16 [8, 3072, 16384], P('expert', 'dp', 'tensor'), may hold values from -0.109375 to 0.109375
- w_down: bfloat16 [8, 3072, 16384], P('expert', 'dp', 'tensor'), may hold values from -0.046875 to 0.046875
Outputs:
- input_grad: bfloat16 [2048, 3072], P(('dp', 'expert', 'tensor'))
- grad_up: bfloat16 [8, 3072, 16384], P('expert', 'dp', 'tensor')
- grad_down: bfloat16 [8, 3072, 16384], P('expert', 'dp', 'tensor')
The draws below stay inside these ranges and needn't reach their ends.
Inputs may be any that keep to these rules, and one draw needn't show every extreme that they name: `expert_ids`: the 2 ids of a token differ. Among the ids of the 128 tokens of one group (aligned blocks of 128 rows) no expert is named more than 36 times, a bound that some block reaches.
All inputs are finite; a program needn't handle non-finite values.
Results may differ from the reference program's by a relative error of at most 0.0057.
Values may be sent and summed in bfloat16 or wider, within the bound.
A program may use at most 128 MiB of HBM per device.

```python
import math
import jax
import jax.numpy as jnp
import numpy as np
from jax import lax

D = 3072
FF = 16384
TOP = 2
TOK_GRP = 128
EXPERTS = 8
CAP = 36
TOKENS = 2048
N_DP = 2
N_EXPERT = 8


def block_scale(key, shape, split, smallest, high):
    level = 1.0
    for position, parts in split:
        steps = jax.random.uniform(jax.random.fold_in(jax.random.fold_in(key, 6), position), (parts,), jnp.float32, smallest / len(split), high / len(split))
        level = level * jnp.repeat(jnp.exp(steps), shape[position] // parts).reshape((-1,) + (1,) * (len(shape) - 1 - position))
    return level


def assign_block(key, own, number, rows, amount, top, reach, skew):
    sequence = jax.random.permutation(key, amount)
    packed, common = portions_of(amount, rows * top, reach, skew, True), portions_of(amount, rows * top, reach, skew, False)
    places = jnp.arange(amount)

    def named(sizes, offset_by):
        used = int((sizes > 0).sum())
        fixed = max(1, used // 4)
        passed = fixed + (places - fixed + offset_by * (used - fixed)) % max(1, amount - fixed)
        return jnp.zeros((amount,), jnp.int32).at[sequence[jnp.where(places < fixed, places, passed)]].set(jnp.asarray(sizes, jnp.int32))

    sizes = jnp.where(number % 4 == 0, named(packed, number // 4), named(common, number - number // 4 - 1))
    mixed = jax.random.permutation(jax.random.fold_in(own, 3), amount)
    source_of, receiver = mixed[0:amount // 2 * 2:2], mixed[1:amount // 2 * 2:2]
    margin = jnp.minimum(sizes[source_of] - 1, reach - sizes[receiver]) // 2
    margin = jnp.where((source_of == sequence[0]) | (receiver == sequence[0]) | (sizes[receiver] == 0), 0, jnp.maximum(margin, 0))
    passed = jax.random.randint(jax.random.fold_in(own, 4), (amount // 2,), 0, 1 << 20) % (margin + 1)
    sizes = sizes.at[source_of].add(-passed).at[receiver].add(passed)
    items = jnp.searchsorted(jnp.cumsum(sizes), jnp.arange(rows * top), side="right").astype(jnp.int32)
    listing = items.reshape(top, rows).T
    listing = listing[jax.random.permutation(jax.random.fold_in(own, 1), rows)]
    offset_by = jax.random.randint(jax.random.fold_in(own, 2), (rows, 1), 0, top)
    return jnp.take_along_axis(listing, (jnp.arange(top)[None, :] + offset_by) % top, axis=1)


def portions_of(count, total, most, skew, full):
    weights = [(1 << 20) // math.isqrt(rank ** skew) + 1 for rank in range(1, count + 1)]
    largest = most if full else min(most, max(-(-total // count), total * weights[0] // sum(weights)))
    least = 1 if total - largest >= count - 1 else 0
    given, rest = [largest] + [least] * (count - 1), total - largest - least * (count - 1)
    while rest > 0:
        free = [i for i in range(1, count) if given[i] < largest] or [i for i in range(1, count) if given[i] < most]
        pool, left = sum([weights[i] for i in free]), rest
        for i in free:
            extra = min(most - given[i], max(1, left * weights[i] // pool), rest)
            given[i] = given[i] + extra
            rest = rest - extra
    return np.array(given)


def bell_draw(stream_key, extent, width, limit, pieces=(), held_as=jnp.bfloat16):
    gain = block_scale(stream_key, extent, pieces, -0.22, 0.18) if pieces else 1.0
    values = jax.random.normal(stream_key, extent, jnp.float32) * width * gain
    return jnp.minimum(jnp.maximum(values, -limit), limit).astype(held_as)


def setup_inputs(seed: int = 0) -> dict:
    keys = jax.random.split(jax.random.key(seed), 7)
    tokens = bell_draw(keys[0], (TOKENS, D), 1.0, 6.0, ((0, 16),))
    cotangent = bell_draw(keys[1], (TOKENS, D), 1.0, 6.0, ((0, 128),))
    expert_ids_keys = jax.random.split(jax.random.fold_in(keys[2], 1), TOKENS // TOK_GRP)
    expert_ids_turns = jax.random.permutation(jax.random.fold_in(keys[2], 3), TOKENS // TOK_GRP)
    expert_ids = jax.vmap(lambda own, number: assign_block(jax.random.fold_in(keys[2], 2), own, number, TOK_GRP, EXPERTS, TOP, CAP, 2))(expert_ids_keys, expert_ids_turns).reshape((TOKENS, TOP))
    route_weight = jnp.clip(0.1 + 0.9 * jax.random.uniform(keys[3], (TOKENS, TOP), jnp.float32) ** block_scale(keys[3], (TOKENS, TOP), ((0, 16),), -0.2, 0.2), 0.1, 1.0)
    w_up = bell_draw(keys[4], (EXPERTS, D, FF), D ** -0.5, 0.109375, ((0, 8), (1, 2), (2, 8)))
    w_down = bell_draw(keys[5], (EXPERTS, D, FF), FF ** -0.5, 0.046875, ((0, 8), (1, 2), (2, 8)))
    return {"tokens": tokens, "cotangent": cotangent, "expert_ids": expert_ids, "route_weight": route_weight, "w_up": w_up, "w_down": w_down}


def expert_pass(inputs):
    rows_x, rows_d, up_w, down_w = inputs
    up_val = jnp.dot(rows_x, up_w, preferred_element_type=jnp.float32)
    sigma = jax.nn.sigmoid(up_val)
    silu = up_val * sigma
    act = silu.astype(jnp.bfloat16)
    d_act = jnp.dot(rows_d, down_w, preferred_element_type=jnp.float32)
    d_up = (d_act * sigma * (1.0 + up_val * (1.0 - sigma))).astype(jnp.bfloat16)
    route_grad = jnp.dot(d_up, up_w.T, preferred_element_type=jnp.float32)
    grad_u = jnp.dot(rows_x.T, d_up, preferred_element_type=jnp.float32).astype(jnp.bfloat16)
    grad_d = jnp.dot(rows_d.T, act, preferred_element_type=jnp.float32).astype(jnp.bfloat16)
    return route_grad, grad_u, grad_d


def reference(tokens, cotangent, expert_ids, route_weight, w_up, w_down):
    ngroups = N_DP * N_EXPERT
    ids = expert_ids.reshape(ngroups, TOK_GRP * TOP).astype(jnp.int32)
    hot = (ids[:, :, None] == jnp.arange(EXPERTS, dtype=jnp.int32)[None, None, :]).astype(jnp.int32)
    before = (jnp.cumsum(hot, axis=1) - hot).astype(jnp.int32)
    slot = jnp.sum(before * hot, axis=2).astype(jnp.int32)
    dest = (ids * CAP + slot).astype(jnp.int32)
    rows_x = jnp.repeat(tokens.reshape(ngroups, TOK_GRP, D), TOP, axis=1)
    rows_c = jnp.repeat(cotangent.reshape(ngroups, TOK_GRP, D), TOP, axis=1).astype(jnp.float32)
    scaled = (route_weight.reshape(ngroups, TOK_GRP * TOP)[:, :, None] * rows_c).astype(jnp.bfloat16)
    owner = jnp.arange(ngroups, dtype=jnp.int32)[:, None]
    buf_x = jnp.zeros((ngroups, EXPERTS * CAP, D), jnp.bfloat16).at[owner, dest].set(rows_x)
    buf_d = jnp.zeros((ngroups, EXPERTS * CAP, D), jnp.bfloat16).at[owner, dest].set(scaled)
    buf_x = jnp.transpose(buf_x.reshape(ngroups, EXPERTS, CAP, D), (1, 0, 2, 3)).reshape(EXPERTS, ngroups * CAP, D)
    buf_d = jnp.transpose(buf_d.reshape(ngroups, EXPERTS, CAP, D), (1, 0, 2, 3)).reshape(EXPERTS, ngroups * CAP, D)
    slots, grad_up, grad_down = lax.map(expert_pass, (buf_x, buf_d, w_up, w_down))
    slots = jnp.transpose(slots.reshape(EXPERTS, ngroups, CAP, D), (1, 0, 2, 3)).reshape(ngroups, EXPERTS * CAP, D)
    picked = jnp.take_along_axis(slots, dest[:, :, None], axis=1)
    input_grad = jnp.sum(picked.reshape(ngroups, TOK_GRP, TOP, D), axis=2).astype(jnp.bfloat16)
    return input_grad.reshape(TOKENS, D), grad_up, grad_down
```

```python
import jax
import jax.numpy as jnp
from jax import lax
from jax.experimental import pallas as pl
from jax.experimental.pallas import tpu as pltpu
from jax.sharding import PartitionSpec as P

CAP = 36
GRP = 128
RC = 4 * CAP
TOKC = 4 * GRP
NF = 4
MESH = pl.DeviceIdType.MESH
BF = jnp.bfloat16
F32 = jnp.float32


def kernel(
    tok,
    cot,
    ids,
    rw,
    wu_hbm,
    wd_hbm,
    out,
    xd_hbm,
    ad_hbm,
    w,
    gat,
    metas,
    slotcol,
    rwcol,
    stage,
    xd,
    own,
    zs,
    zr,
    ad,
    acc,
    c1s,
    c1r,
    c2s,
    res,
    fin_s,
    fin_r,
    w_sem,
    cot_ss,
    cot_rs,
    tok_ss,
    tok_rs,
    met_ss,
    met_rs,
    d_ss,
    d_rs,
    z_ss,
    z_rs,
    c1_ss,
    c1_rs,
    c2_ss,
    c2_rs,
    f_ss,
    f_rs,
    o_sem,
    x_sem,
):
    dp, e, t = lax.axis_index("dp"), lax.axis_index("expert"), lax.axis_index("tensor")
    y, c = e // 2, e % 2
    zlo, x = t // 4, t % 4
    half = w.shape[2]
    fc = w.shape[3]
    xb_w = half // 4

    def at(src, dst, ss, rs, dev):
        return pltpu.make_async_remote_copy(
            src_ref=src, dst_ref=dst, send_sem=ss, recv_sem=rs, device_id=dev, device_id_type=MESH
        )

    def loop(lo, hi, fn):
        def step(i, carry):
            fn(i)
            return carry

        lax.fori_loop(lo, hi, step, 0)

    def w_copy(m, f):
        src = wu_hbm if m == 0 else wd_hbm
        return pltpu.make_async_copy(
            src.at[0, :, pl.ds(pl.multiple_of(f * fc, fc), fc)], w.at[m, f], w_sem.at[m, f]
        )

    for m in range(2):
        for f in range(NF):
            w_copy(m, f).start()

    barrier = pltpu.get_barrier_semaphore()
    me32 = (dp * 8 + t) * 2 + c

    def greet(j):
        i = (me32 + j) % 32
        pl.semaphore_signal(
            barrier, inc=1, device_id=(i // 16, y * 2 + i % 2, (i // 2) % 8), device_id_type=MESH
        )

    loop(1, 32, greet)

    def greet_y(j):
        i = (y * 2 + j) % 8
        pl.semaphore_signal(barrier, inc=1, device_id=(dp, i - i % 2 + (j % 2), t), device_id_type=MESH)

    loop(2, 8, greet_y)
    mine = dp * 2 + c
    metas[mine, 0:2, :] = ids[...].astype(F32)
    metas[mine, 2:4, :] = rw[...]
    pl.semaphore_wait(barrier, 37)

    zn = (1 - dp, 1 - zlo)
    tn = (1 - zlo) * 4 + x

    def met_copy(j):
        dev = ((dp, y * 2 + 1 - c, t), (1 - dp, y * 2 + c, tn), (1 - dp, y * 2 + 1 - c, tn))[j]
        return at(metas.at[mine], metas.at[mine], met_ss.at[j], met_rs.at[mine], dev)

    for j in range(3):
        met_copy(j).start()

    grow = pl.multiple_of(mine * GRP, GRP)
    trow = pl.multiple_of(mine * GRP + t * 16, 16)

    def tok_copy(j):
        h = dp if j == 0 else 1 - dp
        dev = (dp, y * 2, t) if j == 0 else (1 - dp, y * 2, tn)
        return at(
            tok.at[:, pl.ds(pl.multiple_of(h * half, half), half)],
            gat.at[pl.ds(grow, GRP), :],
            tok_ss.at[j],
            tok_rs.at[mine],
            dev,
        )

    me16 = dp * 8 + t
    sidx = mine * 8 + t

    def cot_copy(j):
        i = (me16 + j) % 16
        return at(
            cot.at[:, pl.ds(pl.multiple_of((i // 8) * half, half), half)],
            gat.at[pl.ds(trow, 16), :],
            cot_ss.at[j],
            cot_rs.at[sidx],
            (i // 8, y * 2 + 1, i % 8),
        )

    tok_copy(1).start()
    loop(1, 16, lambda j: cot_copy(j).start())

    @pl.when(c == 1)
    def _():
        tok_copy(0).start()
        gat[pl.ds(trow, 16), :] = cot[:, pl.ds(pl.multiple_of(dp * half, half), half)]

    @pl.when(c == 0)
    def _():
        cot_copy(0).start()
        gat[pl.ds(grow, GRP), :] = tok[:, pl.ds(pl.multiple_of(dp * half, half), half)]

    def met_wait(j):
        g = (mine + j) % 4
        at(metas.at[g], metas.at[g], met_ss.at[0], met_rs.at[g], (dp, y * 2 + 1 - c, t)).wait_recv()

    loop(1, 4, met_wait)
    eio = lax.broadcasted_iota(jnp.int32, (8, GRP), 0).astype(F32)
    tri = (
        lax.broadcasted_iota(jnp.int32, (GRP, GRP), 0) < lax.broadcasted_iota(jnp.int32, (GRP, GRP), 1)
    ).astype(F32).astype(BF)
    for g in range(4):
        mg = metas[g]
        h0 = mg[0:1, :] == eio
        h1 = mg[1:2, :] == eio
        hot = jnp.where(h0, 1.0, jnp.where(h1, 1.0, 0.0))
        slot = jnp.dot(hot.astype(BF), tri, preferred_element_type=F32)
        sc = jnp.where(hot > 0.5, slot + float(g * CAP), -1.0)
        rc = jnp.where(h0, mg[2:3, :], jnp.where(h1, mg[3:4, :], 0.0))
        for k in range(8):
            slotcol[k, 0:1, g * GRP : (g + 1) * GRP] = sc[k : k + 1, :]
            rwcol[k, 0:1, g * GRP : (g + 1) * GRP] = rc[k : k + 1, :]

    def one_hot(ex):
        rio = lax.broadcasted_iota(jnp.int32, (RC, TOKC), 0).astype(F32)
        return rio == slotcol[ex]

    @pl.when(c == 0)
    def _():
        def wait(j):
            g = (mine + j) % 4
            at(
                gat.at[pl.ds(pl.multiple_of(g * GRP, GRP), GRP), :],
                gat.at[pl.ds(pl.multiple_of(g * GRP, GRP), GRP), :],
                tok_ss.at[0],
                tok_rs.at[g],
                (1 - dp, e, tn),
            ).wait_recv()

        loop(1, 4, wait)

    @pl.when(c == 1)
    def _():
        def wait(j):
            i = (sidx + j) % 32
            r = pl.ds(pl.multiple_of(i * 16, 16), 16)
            at(gat.at[r, :], gat.at[r, :], cot_ss.at[0], cot_rs.at[i], (1 - dp, e, tn)).wait_recv()

        loop(1, 32, wait)

    def place(ex, dst):
        hot = one_hot(ex)
        scale = jnp.sum(jnp.where(hot, rwcol[ex], 0.0), axis=1, keepdims=True)
        scale = jnp.where(c == 0, 1.0, scale)
        hot = hot.astype(F32).astype(BF)
        for n in range(4):
            v = jnp.dot(hot, gat[:, n * xb_w : (n + 1) * xb_w], preferred_element_type=F32)
            dst[:, n * xb_w : (n + 1) * xb_w] = (v * scale).astype(BF)

    def d_copy(k, c2):
        return at(
            stage.at[k, c2],
            xd.at[c, k],
            d_ss.at[k, c2],
            d_rs.at[c, k],
            (dp, ((y + 4 - k) % 4) * 2 + c2, t),
        )

    place(y * 2 + 1 - c, stage.at[0, 1 - c])
    d_copy(0, 1 - c).start()
    place(e, xd.at[c, 0])
    for m in range(2):
        for f in range(NF):
            w_copy(m, f).wait()

    def d_wait(m, k):
        at(xd.at[m, k], xd.at[m, k], d_ss.at[0, 0], d_rs.at[m, k], (1 - dp, e, t)).wait_recv()

    d_wait(1 - c, 0)

    other = (1 - dp, e, t)

    def z_copy(k, f):
        return at(zs.at[k, f], zr.at[k, f], z_ss.at[k, f], z_rs.at[k, f], other)

    def x_copy(m, k):
        return pltpu.make_async_copy(
            xd.at[m, k], xd_hbm.at[m, pl.ds(pl.multiple_of(k * RC, RC), RC), :], x_sem.at[m, k]
        )

    def project(k):
        s = k % 2

        def piece(f):
            for m in range(2):
                v = jnp.dot(xd[m, k], w[m, f], preferred_element_type=F32)
                own[s, f, m] = v
                zs[k, f, m] = v.astype(BF)
            z_copy(k, f).start()

        loop(0, NF, piece)
        for m in range(2):
            x_copy(m, k).start()

    project(0)

    def dispatch(i):
        k, c2 = i // 2, i % 2
        place(((y + 4 - k) % 4) * 2 + c2, stage.at[k, c2])
        d_copy(k, c2).start()

    loop(2, 8, dispatch)

    def ad_copy(m, k, f):
        return pltpu.make_async_copy(
            ad.at[k, f, m],
            ad_hbm.at[m, pl.ds(pl.multiple_of(k * RC, RC), RC), pl.ds(pl.multiple_of(f * fc, fc), fc)],
            o_sem.at[m, k, f],
        )

    def c1_copy(k, j):
        xb = (x + j) % 4
        return at(c1s.at[k, xb], c1r.at[k, x], c1_ss.at[k, j], c1_rs.at[k, x], (dp, e, zlo * 4 + xb))

    def c2_copy(k):
        return at(c2s.at[k], res.at[y], c2_ss.at[k], c2_rs.at[y], (dp, ((y + k) % 4) * 2 + c, t))

    def chunk(k):
        @pl.when(k < 3)
        def _():
            d_wait(0, k + 1)
            d_wait(1, k + 1)
            project(k + 1)

        s = k % 2
        acc[...] = jnp.zeros_like(acc)

        def piece(f):
            z_copy(k, f).wait_recv()
            up = own[s, f, 0] + zr[k, f, 0].astype(F32)
            da = own[s, f, 1] + zr[k, f, 1].astype(F32)
            sg = jax.nn.sigmoid(up)
            ad[k, f, 0] = (up * sg).astype(BF)
            du = (da * sg * (1.0 + up * (1.0 - sg))).astype(BF)
            ad[k, f, 1] = du
            ad_copy(0, k, f).start()
            ad_copy(1, k, f).start()
            for n in range(4):
                acc[n] += lax.dot_general(
                    du,
                    w[0, f, n * xb_w : (n + 1) * xb_w, :],
                    (((1,), (1,)), ((), ())),
                    preferred_element_type=F32,
                )

        loop(0, NF, piece)

        def send(j):
            xb = (x + j) % 4
            c1s[k, xb] = acc[xb].astype(BF)
            c1_copy(k, j).start()

        loop(1, 4, send)
        total = acc[x]
        for j in range(1, 4):
            xs = (x + j) % 4
            at(c1r.at[k, xs], c1r.at[k, xs], c1_ss.at[0, 0], c1_rs.at[k, xs], other).wait_recv()
            total += c1r[k, xs].astype(F32)

        @pl.when(k == 0)
        def _():
            res[y] = total.astype(BF)

        @pl.when(k > 0)
        def _():
            c2s[k] = total.astype(BF)
            c2_copy(k).start()

    loop(0, 4, chunk)

    def res_wait(k):
        i = (y + 4 - k) % 4
        at(res.at[i], res.at[i], c2_ss.at[0], c2_rs.at[i], other).wait_recv()

    loop(1, 4, res_wait)
    for g in range(4):
        total = jnp.zeros((GRP, xb_w), F32)
        for k in range(4):
            hot = lax.broadcasted_iota(jnp.int32, (RC, GRP), 0).astype(F32) == slotcol[
                k * 2 + c, :, g * GRP : (g + 1) * GRP
            ]
            total += lax.dot_general(
                hot.astype(F32).astype(BF), res[k], (((0,), (0,)), ((), ())), preferred_element_type=F32
            )
        fin_s[g * GRP : (g + 1) * GRP, :] = total.astype(fin_s.dtype)

    spot = (dp * 4 + x) * 4 + zlo * 2 + c

    def f_copy(j):
        i = (me32 + j) % 32
        d2, t2, c2 = i // 16, (i // 2) % 8, i % 2
        row = pl.multiple_of((d2 * 2 + c2) * GRP + t2 * 16, 16)
        return at(fin_s.at[pl.ds(row, 16), :], fin_r.at[spot], f_ss.at[j], f_rs.at[spot], (d2, y * 2 + c2, t2))

    loop(1, 32, lambda j: f_copy(j).start())
    fin_r[spot] = fin_s[pl.ds(pl.multiple_of(mine * GRP + t * 16, 16), 16), :]

    def f_wait(j):
        i = (spot + j) % 32
        at(fin_r.at[i], fin_r.at[i], f_ss.at[0], f_rs.at[i], other).wait_recv()

    loop(1, 32, f_wait)
    for b in range(8):
        v = fin_r[b * 4].astype(F32)
        for p in range(1, 4):
            v += fin_r[b * 4 + p].astype(F32)
        out[:, b * xb_w : (b + 1) * xb_w] = v.astype(BF)

    for j in range(3):
        met_copy(j).wait_send()
    tok_copy(1).wait_send()
    loop(1, 16, lambda j: cot_copy(j).wait_send())

    @pl.when(c == 1)
    def _():
        tok_copy(0).wait_send()

    @pl.when(c == 0)
    def _():
        cot_copy(0).wait_send()

    d_copy(0, 1 - c).wait_send()
    loop(2, 8, lambda i: d_copy(i // 2, i % 2).wait_send())

    def drain(i):
        k, f = i // NF, i % NF
        z_copy(k, f).wait_send()
        ad_copy(0, k, f).wait()
        ad_copy(1, k, f).wait()

    loop(0, 4 * NF, drain)
    loop(0, 12, lambda i: c1_copy(i // 3, 1 + i % 3).wait_send())
    loop(1, 4, lambda k: c2_copy(k).wait_send())
    loop(1, 32, lambda j: f_copy(j).wait_send())

    def x_drain(k):
        x_copy(0, k).wait()
        x_copy(1, k).wait()

    loop(0, 4, x_drain)


def shards(tokens, cotangent, expert_ids, route_weight, w_up, w_down):
    half, ff = w_up.shape[1], w_up.shape[2]
    rows = 4 * RC
    fc = ff // NF
    xb_w = half // 4
    vmem = pl.BlockSpec(memory_space=pltpu.VMEM)
    hbm = pl.BlockSpec(memory_space=pl.ANY)
    dma = pltpu.SemaphoreType.DMA
    out, xd, ad = pl.pallas_call(
        kernel,
        out_shape=(
            jax.ShapeDtypeStruct(cotangent.shape, BF),
            jax.ShapeDtypeStruct((2, rows, half), BF),
            jax.ShapeDtypeStruct((2, rows, ff), BF),
        ),
        in_specs=[vmem] * 4 + [hbm] * 2,
        out_specs=(vmem, hbm, hbm),
        scratch_shapes=[
            pltpu.VMEM((2, NF, half, fc), BF),
            pltpu.VMEM((TOKC, half), BF),
            pltpu.VMEM((4, 4, GRP), F32),
            pltpu.VMEM((8, 1, TOKC), F32),
            pltpu.VMEM((8, 1, TOKC), F32),
            pltpu.VMEM((4, 2, RC, half), BF),
            pltpu.VMEM((2, 4, RC, half), BF),
            pltpu.VMEM((2, NF, 2, RC, fc), F32),
            pltpu.VMEM((4, NF, 2, RC, fc), BF),
            pltpu.VMEM((4, NF, 2, RC, fc), BF),
            pltpu.VMEM((4, NF, 2, RC, fc), BF),
            pltpu.VMEM((4, RC, xb_w), F32),
            pltpu.VMEM((4, 4, RC, xb_w), BF),
            pltpu.VMEM((4, 4, RC, xb_w), BF),
            pltpu.VMEM((4, RC, xb_w), BF),
            pltpu.VMEM((4, RC, xb_w), BF),
            pltpu.VMEM((TOKC, xb_w), BF),
            pltpu.VMEM((32, 16, xb_w), BF),
            dma((2, NF)),
            dma((16,)),
            dma((32,)),
            dma((2,)),
            dma((4,)),
            dma((3,)),
            dma((4,)),
            dma((4, 2)),
            dma((2, 4)),
            dma((4, NF)),
            dma((4, NF)),
            dma((4, 4)),
            dma((4, 4)),
            dma((4,)),
            dma((4,)),
            dma((32,)),
            dma((32,)),
            dma((2, 4, NF)),
            dma((2, 4)),
        ],
        compiler_params=pltpu.CompilerParams(
            collective_id=0, has_side_effects=True, vmem_limit_bytes=58 * 2**20
        ),
        cost_estimate=pl.CostEstimate(
            flops=6 * rows * half * ff, bytes_accessed=4 * half * ff, transcendentals=rows * ff
        ),
    )(tokens, cotangent, expert_ids.T, route_weight.T, w_up, w_down)

    def grad(left, right):
        return lax.dot_general(
            left, right, (((0,), (0,)), ((), ())), preferred_element_type=F32
        ).astype(BF)[None]

    return out, grad(xd[0], ad[1]), grad(xd[1], ad[0])


def solution(mesh):
    placed = (
        P(("dp", "expert"), None),
        P(("dp", "expert", "tensor"), None),
        P(("dp", "expert"), None),
        P(("dp", "expert"), None),
        P("expert", "dp", "tensor"),
        P("expert", "dp", "tensor"),
    )
    return jax.shard_map(
        shards,
        mesh=mesh,
        in_specs=placed,
        out_specs=(
            P(("dp", "expert", "tensor"), None),
            P("expert", "dp", "tensor"),
            P("expert", "dp", "tensor"),
        ),
        check_vma=False,
    )
```

```python
import jax
import jax.numpy as jnp
from jax import lax
from jax.experimental import pallas as pl
from jax.experimental.pallas import tpu as pltpu
from jax.sharding import PartitionSpec as P

CAP = 36
GRP = 128
RC = 4 * CAP
TOKC = 4 * GRP
PR = 80
NF = 4
MESH = pl.DeviceIdType.MESH
BF = jnp.bfloat16
F32 = jnp.float32


def kernel(
    tok,
    cot,
    ids,
    rw,
    wu_hbm,
    wd_hbm,
    out,
    xd_hbm,
    ad_hbm,
    gp_hbm,
    w,
    gat,
    metas,
    slotcol,
    rwcol,
    stage,
    xd,
    own,
    zs,
    zr,
    ad,
    acc,
    c1s,
    c1r,
    c2s,
    res,
    fin_s,
    fin_r,
    unhot,
    gs,
    w_sem,
    cot_ss,
    fwd_ss,
    cot_rs,
    tok_ss,
    tok_rs,
    met_ss,
    met_rs,
    d_ss,
    d_rs,
    z_ss,
    z_rs,
    c1_ss,
    c1_rs,
    c2_ss,
    c2_rs,
    f_ss,
    f_rs,
    o_sem,
    x_sem,
    g_sem,
):
    dp, e, t = lax.axis_index("dp"), lax.axis_index("expert"), lax.axis_index("tensor")
    y, c = e // 2, e % 2
    zlo, x = t // 4, t % 4
    z = dp * 2 + zlo
    half = w.shape[2]
    fc = w.shape[3]
    xb_w = half // 4

    def at(src, dst, ss, rs, dev):
        return pltpu.make_async_remote_copy(
            src_ref=src, dst_ref=dst, send_sem=ss, recv_sem=rs, device_id=dev, device_id_type=MESH
        )

    def loop(lo, hi, fn):
        def step(i, carry):
            fn(i)
            return carry

        lax.fori_loop(lo, hi, step, 0)

    def w_copy(m, f):
        src = wu_hbm if m == 0 else wd_hbm
        return pltpu.make_async_copy(
            src.at[0, :, pl.ds(pl.multiple_of(f * fc, fc), fc)], w.at[m, f], w_sem.at[m, f]
        )

    for m in range(2):
        for f in range(NF):
            w_copy(m, f).start()

    barrier = pltpu.get_barrier_semaphore()
    me16 = dp * 8 + t

    def greet(d, ex, tt):
        pl.semaphore_signal(barrier, inc=1, device_id=(d, ex, tt), device_id_type=MESH)

    def greet_plane(j):
        i = (me16 + j) % 16
        greet(i // 8, e, i % 8)

    loop(1, 16, greet_plane)
    for j in range(4):
        zz = (z + j) % 4
        greet(zz // 2, y * 2 + 1 - c, (zz % 2) * 4 + x)
    for j in range(1, 4):
        for c2 in range(2):
            greet(dp, ((y + j) % 4) * 2 + c2, t)
    mine = c * 2 + dp
    metas[mine, 0:2, :] = ids[...].astype(F32)
    metas[mine, 2:4, :] = rw[...]
    pl.semaphore_wait(barrier, 25)

    tn = (1 - zlo) * 4 + x

    def met_copy(j):
        dev = ((dp, y * 2 + 1 - c, t), (1 - dp, y * 2 + c, tn), (1 - dp, y * 2 + 1 - c, tn))[j]
        return at(metas.at[mine], metas.at[mine], met_ss.at[j], met_rs.at[mine], dev)

    for j in range(3):
        met_copy(j).start()

    grow = pl.multiple_of(mine * GRP, GRP)
    trow = pl.multiple_of(mine * GRP + t * 16, 16)

    def tok_copy(j):
        h = dp if j == 0 else 1 - dp
        dev = (dp, y * 2, t) if j == 0 else (1 - dp, y * 2, tn)
        return at(
            tok.at[:, pl.ds(pl.multiple_of(h * half, half), half)],
            gat.at[pl.ds(grow, GRP), :],
            tok_ss.at[j],
            tok_rs.at[mine],
            dev,
        )

    sidx = mine * 8 + t

    def cot_copy(j):
        zz = (z + j) % 4
        return at(
            cot.at[:, pl.ds(pl.multiple_of((zz // 2) * half, half), half)],
            gat.at[pl.ds(trow, 16), :],
            cot_ss.at[j],
            cot_rs.at[sidx],
            (zz // 2, y * 2 + 1, (zz % 2) * 4 + x),
        )

    def shard(q, xs):
        zz = (z + q // 2) % 4
        return (((c + q) % 2) * 2 + zz // 2) * 8 + (zz % 2) * 4 + xs

    def rows_of(i):
        return gat.at[pl.ds(pl.multiple_of(i * 16, 16), 16), :]

    def fwd_copy(q, j):
        i = shard(q, x)
        return at(
            rows_of(i), rows_of(i), fwd_ss.at[q, j - 1], cot_rs.at[i], (dp, e, zlo * 4 + (x + j) % 4)
        )

    def cot_wait(i):
        at(rows_of(i), rows_of(i), cot_ss.at[0], cot_rs.at[i], (1 - dp, e, tn)).wait_recv()

    for j in range(1, 4):
        cot_copy(j).start()

    @pl.when(c == 0)
    def _():
        cot_copy(0).start()

    tok_copy(1).start()

    @pl.when(c == 0)
    def _():
        gat[pl.ds(grow, GRP), :] = tok[:, pl.ds(pl.multiple_of(dp * half, half), half)]

    @pl.when(c == 1)
    def _():
        tok_copy(0).start()
        gat[pl.ds(trow, 16), :] = cot[:, pl.ds(pl.multiple_of(dp * half, half), half)]

        def forward(q):
            @pl.when(q > 0)
            def _():
                cot_wait(shard(q, x))

            for j in range(1, 4):
                fwd_copy(q, j).start()

        loop(0, 8, forward)

    def met_wait(j):
        g = (mine + j) % 4
        at(metas.at[g], metas.at[g], met_ss.at[0], met_rs.at[g], (dp, y * 2 + 1 - c, t)).wait_recv()

    loop(1, 4, met_wait)
    eio = lax.broadcasted_iota(jnp.int32, (8, GRP), 0).astype(F32)
    tri = (
        lax.broadcasted_iota(jnp.int32, (GRP, GRP), 0) < lax.broadcasted_iota(jnp.int32, (GRP, GRP), 1)
    ).astype(F32).astype(BF)
    for g in range(4):
        mg = metas[g]
        h0 = mg[0:1, :] == eio
        h1 = mg[1:2, :] == eio
        hot = jnp.where(h0, 1.0, jnp.where(h1, 1.0, 0.0))
        slot = jnp.dot(hot.astype(BF), tri, preferred_element_type=F32)
        sc = jnp.where(hot > 0.5, slot + float(g * CAP), -1.0)
        rc = jnp.where(h0, mg[2:3, :], jnp.where(h1, mg[3:4, :], 0.0))
        for k in range(8):
            slotcol[k, 0:1, g * GRP : (g + 1) * GRP] = sc[k : k + 1, :]
            rwcol[k, 0:1, g * GRP : (g + 1) * GRP] = rc[k : k + 1, :]

    def one_hot(ex):
        rio = lax.broadcasted_iota(jnp.int32, (RC, TOKC), 0).astype(F32)
        return rio == slotcol[ex]

    @pl.when(c == 0)
    def _():
        def wait(j):
            g = (mine + j) % 4
            at(
                gat.at[pl.ds(pl.multiple_of(g * GRP, GRP), GRP), :],
                gat.at[pl.ds(pl.multiple_of(g * GRP, GRP), GRP), :],
                tok_ss.at[0],
                tok_rs.at[g],
                (1 - dp, e, tn),
            ).wait_recv()

        loop(1, 4, wait)

    @pl.when(c == 1)
    def _():
        loop(0, 24, lambda i: cot_wait(shard(i % 8, (x + 1 + i // 8) % 4)))

    def place(ex, dst):
        hot = one_hot(ex)
        scale = jnp.sum(jnp.where(hot, rwcol[ex], 0.0), axis=1, keepdims=True)
        scale = jnp.where(c == 0, 1.0, scale)
        hot = hot.astype(F32).astype(BF)
        for n in range(4):
            v = jnp.dot(hot, gat[:, n * xb_w : (n + 1) * xb_w], preferred_element_type=F32)
            dst[:, n * xb_w : (n + 1) * xb_w] = (v * scale).astype(BF)

    def d_copy(k, c2):
        return at(
            stage.at[k, c2],
            xd.at[c, k],
            d_ss.at[k, c2],
            d_rs.at[c, k],
            (dp, ((y + 4 - k) % 4) * 2 + c2, t),
        )

    place(y * 2 + 1 - c, stage.at[0, 1 - c])
    d_copy(0, 1 - c).start()
    place(e, xd.at[c, 0])
    for m in range(2):
        for f in range(NF):
            w_copy(m, f).wait()

    def d_wait(m, k):
        at(xd.at[m, k], xd.at[m, k], d_ss.at[0, 0], d_rs.at[m, k], (1 - dp, e, t)).wait_recv()

    d_wait(1 - c, 0)

    other = (1 - dp, e, t)

    def z_copy(k, f):
        return at(zs.at[k, f], zr.at[k, f], z_ss.at[k, f], z_rs.at[k, f], other)

    def x_copy(m, k):
        return pltpu.make_async_copy(
            xd.at[m, k], xd_hbm.at[m], x_sem.at[m]
        )

    def project(k):
        s = k % 2

        def piece(f):
            for m in range(2):
                v = jnp.dot(xd[m, k], w[m, f], preferred_element_type=F32)
                own[s, f, m] = v
                zs[k, f, m] = v.astype(BF)
            z_copy(k, f).start()

        loop(0, NF, piece)

    project(0)

    def dispatch(i):
        k, c2 = i // 2, i % 2
        place(((y + 4 - k) % 4) * 2 + c2, stage.at[k, c2])
        d_copy(k, c2).start()

    loop(2, 8, dispatch)
    cols = pl.ds(pl.multiple_of(c * 2 * GRP, 2 * GRP), 2 * GRP)
    rio = lax.broadcasted_iota(jnp.int32, (8, PR, 2 * GRP), 1) + c * (2 * CAP)
    hot = jnp.where(rio.astype(F32) == slotcol[:, :, cols], 1.0, 0.0).reshape(8 * PR, 2 * GRP)
    unhot[...] = hot.T.astype(BF)

    def ad_copy(m, k, f):
        return pltpu.make_async_copy(
            ad.at[k, f, m],
            ad_hbm.at[m, :, pl.ds(pl.multiple_of(f * fc, fc), fc)],
            o_sem.at[m, f],
        )

    def c1_copy(k, j):
        xb = (x + j) % 4
        return at(c1s.at[k, xb], c1r.at[k, x], c1_ss.at[k, j], c1_rs.at[k, x], (dp, e, zlo * 4 + xb))

    def c2_copy(k, c2):
        dev = (dp, ((y + k) % 4) * 2 + c2, t)
        return at(c2s.at[k, c2], res.at[e], c2_ss.at[k, c2], c2_rs.at[e], dev)

    def g_copy(i):
        m, f = i // NF, i % NF
        return pltpu.make_async_copy(
            gs.at[i % 2],
            gp_hbm.at[m, :, pl.ds(pl.multiple_of(f * fc, fc), fc)],
            g_sem.at[i],
        )

    def gradient(i):
        m, f = i // NF, i % NF

        @pl.when(i >= 2)
        def _():
            g_copy(i - 2).wait()

        right = ad[0:3, f, 1 - m].reshape(3 * RC, fc)
        for n in range(4):
            left = xd[m, 0:3, :, n * xb_w : (n + 1) * xb_w].reshape(3 * RC, xb_w)
            v = lax.dot_general(left, right, (((0,), (0,)), ((), ())), preferred_element_type=F32)
            gs[i % 2, n * xb_w : (n + 1) * xb_w, :] = v.astype(BF)
        g_copy(i).start()

    def chunk(k):
        @pl.when(k < 3)
        def _():
            d_wait(0, k + 1)
            d_wait(1, k + 1)
            project(k + 1)

        @pl.when(k == 2)
        def _():
            x_copy(0, 3).start()
            x_copy(1, 3).start()

        s = k % 2
        acc[...] = jnp.zeros_like(acc)

        def piece(f):
            z_copy(k, f).wait_recv()
            up = own[s, f, 0] + zr[k, f, 0].astype(F32)
            da = own[s, f, 1] + zr[k, f, 1].astype(F32)
            sg = jax.nn.sigmoid(up)
            ad[k, f, 0] = (up * sg).astype(BF)
            du = (da * sg * (1.0 + up * (1.0 - sg))).astype(BF)
            ad[k, f, 1] = du

            @pl.when(k == 3)
            def _():
                ad_copy(0, 3, f).start()
                ad_copy(1, 3, f).start()

            for n in range(4):
                acc[n] += lax.dot_general(
                    du,
                    w[0, f, n * xb_w : (n + 1) * xb_w, :],
                    (((1,), (1,)), ((), ())),
                    preferred_element_type=F32,
                )

        loop(0, NF, piece)

        def send(j):
            xb = (x + j) % 4
            c1s[k, xb] = acc[xb].astype(BF)
            c1_copy(k, j).start()

        loop(1, 4, send)

        @pl.when(k == 2)
        def _():
            loop(0, 2 * NF, gradient)

        total = acc[x]
        for j in range(1, 4):
            xs = (x + j) % 4
            at(c1r.at[k, xs], c1r.at[k, xs], c1_ss.at[0, 0], c1_rs.at[k, xs], other).wait_recv()
            total += c1r[k, xs].astype(F32)

        for c2 in range(2):
            part = total[c2 * 2 * CAP : (c2 + 1) * 2 * CAP, :]
            part = jnp.concatenate([part, jnp.zeros((PR - 2 * CAP, xb_w), F32)], axis=0).astype(BF)
            own_rows = jnp.logical_and(k == 0, c == c2)

            @pl.when(own_rows)
            def _():
                res[e] = part

            @pl.when(jnp.logical_not(own_rows))
            def _():
                c2s[k, c2] = part
                c2_copy(k, c2).start()

    loop(0, 4, chunk)

    def res_wait(j):
        i = (e + j) % 8
        at(res.at[i], res.at[i], c2_ss.at[0, 0], c2_rs.at[i], other).wait_recv()

    loop(1, 8, res_wait)
    back = res[...].reshape(8 * PR, xb_w)
    fin_s[...] = jnp.dot(unhot[...], back, preferred_element_type=F32).astype(BF)

    spot = (dp * 4 + x) * 2 + zlo

    def f_copy(j):
        i = (me16 + j) % 16
        row = pl.multiple_of(i * 16, 16)
        return at(fin_s.at[pl.ds(row, 16), :], fin_r.at[spot], f_ss.at[j], f_rs.at[spot], (i // 8, e, i % 8))

    loop(1, 16, lambda j: f_copy(j).start())
    fin_r[spot] = fin_s[pl.ds(pl.multiple_of(me16 * 16, 16), 16), :]

    def f_wait(j):
        i = (spot + j) % 16
        at(fin_r.at[i], fin_r.at[i], f_ss.at[0], f_rs.at[i], other).wait_recv()

    loop(1, 16, f_wait)
    for b in range(8):
        v = fin_r[b * 2].astype(F32) + fin_r[b * 2 + 1].astype(F32)
        out[:, b * xb_w : (b + 1) * xb_w] = v.astype(BF)

    for j in range(3):
        met_copy(j).wait_send()
    tok_copy(1).wait_send()
    loop(1, 4, lambda j: cot_copy(j).wait_send())

    @pl.when(c == 1)
    def _():
        tok_copy(0).wait_send()
        loop(0, 24, lambda i: fwd_copy(i // 3, 1 + i % 3).wait_send())

    @pl.when(c == 0)
    def _():
        cot_copy(0).wait_send()

    d_copy(0, 1 - c).wait_send()
    loop(2, 8, lambda i: d_copy(i // 2, i % 2).wait_send())

    loop(0, 4 * NF, lambda i: z_copy(i // NF, i % NF).wait_send())
    loop(0, 12, lambda i: c1_copy(i // 3, 1 + i % 3).wait_send())
    c2_copy(0, 1 - c).wait_send()
    loop(2, 8, lambda i: c2_copy(i // 2, i % 2).wait_send())
    loop(1, 16, lambda j: f_copy(j).wait_send())
    for m in range(2):
        for f in range(NF):
            ad_copy(m, 3, f).wait()
        x_copy(m, 3).wait()
    g_copy(2 * NF - 2).wait()
    g_copy(2 * NF - 1).wait()


def shards(tokens, cotangent, expert_ids, route_weight, w_up, w_down):
    half, ff = w_up.shape[1], w_up.shape[2]
    rows = 4 * RC
    fc = ff // NF
    xb_w = half // 4
    vmem = pl.BlockSpec(memory_space=pltpu.VMEM)
    hbm = pl.BlockSpec(memory_space=pl.ANY)
    dma = pltpu.SemaphoreType.DMA
    out, xd, ad, gp = pl.pallas_call(
        kernel,
        out_shape=(
            jax.ShapeDtypeStruct(cotangent.shape, BF),
            jax.ShapeDtypeStruct((2, RC, half), BF),
            jax.ShapeDtypeStruct((2, RC, ff), BF),
            jax.ShapeDtypeStruct((2, half, ff), BF),
        ),
        in_specs=[vmem] * 4 + [hbm] * 2,
        out_specs=(vmem, hbm, hbm, hbm),
        scratch_shapes=[
            pltpu.VMEM((2, NF, half, fc), BF),
            pltpu.VMEM((TOKC, half), BF),
            pltpu.VMEM((4, 4, GRP), F32),
            pltpu.VMEM((8, 1, TOKC), F32),
            pltpu.VMEM((8, 1, TOKC), F32),
            pltpu.VMEM((4, 2, RC, half), BF),
            pltpu.VMEM((2, 4, RC, half), BF),
            pltpu.VMEM((2, NF, 2, RC, fc), F32),
            pltpu.VMEM((4, NF, 2, RC, fc), BF),
            pltpu.VMEM((4, NF, 2, RC, fc), BF),
            pltpu.VMEM((4, NF, 2, RC, fc), BF),
            pltpu.VMEM((4, RC, xb_w), F32),
            pltpu.VMEM((4, 4, RC, xb_w), BF),
            pltpu.VMEM((4, 4, RC, xb_w), BF),
            pltpu.VMEM((4, 2, PR, xb_w), BF),
            pltpu.VMEM((8, PR, xb_w), BF),
            pltpu.VMEM((2 * GRP, xb_w), BF),
            pltpu.VMEM((16, 16, xb_w), BF),
            pltpu.VMEM((2 * GRP, 8 * PR), BF),
            pltpu.VMEM((2, half, fc), BF),
            dma((2, NF)),
            dma((4,)),
            dma((8, 3)),
            dma((32,)),
            dma((2,)),
            dma((4,)),
            dma((3,)),
            dma((4,)),
            dma((4, 2)),
            dma((2, 4)),
            dma((4, NF)),
            dma((4, NF)),
            dma((4, 4)),
            dma((4, 4)),
            dma((4, 2)),
            dma((8,)),
            dma((16,)),
            dma((16,)),
            dma((2, NF)),
            dma((2,)),
            dma((2 * NF,)),
        ],
        compiler_params=pltpu.CompilerParams(
            collective_id=0, has_side_effects=True, vmem_limit_bytes=58 * 2**20
        ),
        cost_estimate=pl.CostEstimate(
            flops=6 * rows * half * ff, bytes_accessed=4 * half * ff, transcendentals=rows * ff
        ),
    )(tokens, cotangent, expert_ids.T, route_weight.T, w_up, w_down)

    def grad(part, left, right):
        last = lax.dot_general(left, right, (((0,), (0,)), ((), ())), preferred_element_type=F32)
        return (part.astype(F32) + last).astype(BF)[None]

    return out, grad(gp[0], xd[0], ad[1]), grad(gp[1], xd[1], ad[0])


def solution(mesh):
    placed = (
        P(("dp", "expert"), None),
        P(("dp", "expert", "tensor"), None),
        P(("dp", "expert"), None),
        P(("dp", "expert"), None),
        P("expert", "dp", "tensor"),
        P("expert", "dp", "tensor"),
    )
    return jax.shard_map(
        shards,
        mesh=mesh,
        in_specs=placed,
        out_specs=(
            P(("dp", "expert", "tensor"), None),
            P("expert", "dp", "tensor"),
            P("expert", "dp", "tensor"),
        ),
        check_vma=False,
    )
```

```python
import jax
import jax.numpy as jnp
from jax import lax
from jax.experimental import pallas as pl
from jax.experimental.pallas import tpu as pltpu
from jax.sharding import PartitionSpec as P

CAP = 36
GRP = 128
RC = 4 * CAP
TOKC = 4 * GRP
PR = 80
NG = 4
NF = 4
WHOLE = (0, RC)
PLACED = ((0, 64), (64, 80))
EARLY = (0, 128)
LATE = (128, 16)
FIN = RC + LATE[1]
UNITS = ((0, (0, 64)), (0, (64, 64)), (1, WHOLE), (2, WHOLE), (3, WHOLE), (0, LATE))
SUMS = ((0, EARLY), (1, WHOLE), (2, WHOLE), (3, WHOLE), (0, (RC, LATE[1])))
AWAY = (0, 1, 3, 2)
MESH = pl.DeviceIdType.MESH
BF = jnp.bfloat16
F32 = jnp.float32


def kernel(
    tok,
    cot,
    ids,
    rw,
    wu_hbm,
    wd_hbm,
    out,
    xd_hbm,
    ad_hbm,
    gu_hbm,
    gd_hbm,
    w,
    gat,
    metas,
    slotcol,
    rwcol,
    xd,
    own,
    zs,
    zr,
    ad,
    acc,
    c1s,
    c1r,
    c2s,
    res,
    fin_s,
    fin_r,
    unhot,
    held,
    turned,
    gs,
    w_sem,
    cot_ss,
    fwd_ss,
    cot_rs,
    tok_ss,
    tok_rs,
    met_ss,
    met_rs,
    d0_ss,
    d0_rs,
    d_ss,
    d_rs,
    z_ss,
    z_rs,
    c1_ss,
    c1_rs,
    c2_ss,
    c2_rs,
    f_ss,
    f_rs,
    o_sem,
    x_sem,
    g_sem,
):
    dp, e, t = lax.axis_index("dp"), lax.axis_index("expert"), lax.axis_index("tensor")
    y, c = e // 2, e % 2
    zlo, x = t // 4, t % 4
    z = dp * 2 + zlo
    half = w.shape[2]
    fc = w.shape[3]
    xb_w = half // 4
    gc = NF * fc // NG

    def at(src, dst, ss, rs, dev):
        return pltpu.make_async_remote_copy(
            src_ref=src, dst_ref=dst, send_sem=ss, recv_sem=rs, device_id=dev, device_id_type=MESH
        )

    def loop(lo, hi, fn):
        def step(i, carry):
            fn(i)
            return carry

        lax.fori_loop(lo, hi, step, 0)

    def w_copy(m, f):
        src = wu_hbm if m == 0 else wd_hbm
        return pltpu.make_async_copy(
            src.at[0, :, pl.ds(pl.multiple_of(f * fc, fc), fc)], w.at[m, f], w_sem.at[m, f]
        )

    for m in range(2):
        for f in range(NF):
            w_copy(m, f).start()

    barrier = pltpu.get_barrier_semaphore()
    me16 = dp * 8 + t

    def greet(d, ex, tt):
        pl.semaphore_signal(barrier, inc=1, device_id=(d, ex, tt), device_id_type=MESH)

    def greet_plane(j):
        i = (me16 + j) % 16
        greet(i // 8, e, i % 8)

    loop(1, 16, greet_plane)
    for j in range(4):
        zz = (z + j) % 4
        greet(zz // 2, y * 2 + 1 - c, (zz % 2) * 4 + x)
    for j in range(1, 4):
        for c2 in range(2):
            greet(dp, ((y + j) % 4) * 2 + c2, t)
    mine = c * 2 + dp
    metas[mine, 0:2, :] = ids[...].astype(F32)
    metas[mine, 2:4, :] = rw[...]
    pl.semaphore_wait(barrier, 25)

    tn = (1 - zlo) * 4 + x

    def met_copy(j):
        dev = ((dp, y * 2 + 1 - c, t), (1 - dp, y * 2 + c, tn), (1 - dp, y * 2 + 1 - c, tn))[j]
        return at(metas.at[mine], metas.at[mine], met_ss.at[j], met_rs.at[mine], dev)

    for j in range(3):
        met_copy(j).start()

    grow = pl.multiple_of(mine * GRP, GRP)
    trow = pl.multiple_of(mine * GRP + t * 16, 16)

    def tok_copy(j):
        h = dp if j == 0 else 1 - dp
        dev = (dp, y * 2, t) if j == 0 else (1 - dp, y * 2, tn)
        return at(
            tok.at[:, pl.ds(pl.multiple_of(h * half, half), half)],
            gat.at[pl.ds(grow, GRP), :],
            tok_ss.at[j],
            tok_rs.at[mine],
            dev,
        )

    sidx = mine * 8 + t

    def cot_copy(j):
        zz = (z + j) % 4
        return at(
            cot.at[:, pl.ds(pl.multiple_of((zz // 2) * half, half), half)],
            gat.at[pl.ds(trow, 16), :],
            cot_ss.at[j],
            cot_rs.at[sidx],
            (zz // 2, y * 2 + 1, (zz % 2) * 4 + x),
        )

    def shard(q, xs):
        zz = (z + q) % 4
        return ((q // 4) * 2 + zz // 2) * 8 + (zz % 2) * 4 + xs

    def rows_of(i):
        return gat.at[pl.ds(pl.multiple_of(i * 16, 16), 16), :]

    def fwd_copy(q, j):
        i = shard(q, x)
        return at(
            rows_of(i), rows_of(i), fwd_ss.at[q, j - 1], cot_rs.at[i], (dp, e, zlo * 4 + (x + j) % 4)
        )

    def cot_wait(i):
        at(rows_of(i), rows_of(i), cot_ss.at[0], cot_rs.at[i], (1 - dp, e, tn)).wait_recv()

    for j in range(1, 4):
        cot_copy(j).start()

    @pl.when(c == 0)
    def _():
        cot_copy(0).start()
        tok_copy(1).start()
        gat[pl.ds(grow, GRP), :] = tok[:, pl.ds(pl.multiple_of(dp * half, half), half)]

    @pl.when(c == 1)
    def _():
        gat[pl.ds(trow, 16), :] = cot[:, pl.ds(pl.multiple_of(dp * half, half), half)]

        def forward(q):
            @pl.when(q != 4)
            def _():
                cot_wait(shard(q, x))

            for j in range(1, 4):
                fwd_copy(q, j).start()

        loop(0, 8, forward)
        tok_copy(1).start()
        tok_copy(0).start()

    def met_wait(j):
        g = (mine + j) % 4
        at(metas.at[g], metas.at[g], met_ss.at[0], met_rs.at[g], (dp, y * 2 + 1 - c, t)).wait_recv()

    loop(1, 4, met_wait)
    eio = lax.broadcasted_iota(jnp.int32, (8, GRP), 0).astype(F32)
    tri = (
        lax.broadcasted_iota(jnp.int32, (GRP, GRP), 0) < lax.broadcasted_iota(jnp.int32, (GRP, GRP), 1)
    ).astype(F32).astype(BF)
    for g in range(4):
        mg = metas[g]
        h0 = mg[0:1, :] == eio
        h1 = mg[1:2, :] == eio
        hot = jnp.where(h0, 1.0, jnp.where(h1, 1.0, 0.0))
        slot = jnp.dot(hot.astype(BF), tri, preferred_element_type=F32)
        sc = jnp.where(hot > 0.5, slot + float(g * CAP), -1.0)
        rc = jnp.where(h0, mg[2:3, :], jnp.where(h1, mg[3:4, :], 0.0))
        for k in range(8):
            slotcol[k, 0:1, g * GRP : (g + 1) * GRP] = sc[k : k + 1, :]
            rwcol[k, 0:1, g * GRP : (g + 1) * GRP] = rc[k : k + 1, :]

    def tok_wait(g):
        group = gat.at[pl.ds(pl.multiple_of(g * GRP, GRP), GRP), :]
        at(group, group, tok_ss.at[0], tok_rs.at[g], (1 - dp, e, tn)).wait_recv()

    def gathered(c2):
        @pl.when(c == 0)
        def _():
            if c2 == 0:
                tok_wait(1 - dp)
            else:
                tok_wait(2)
                tok_wait(3)

        @pl.when(c == 1)
        def _():
            loop(0, 12, lambda i: cot_wait(shard(c2 * 4 + i % 4, (x + 1 + i // 4) % 4)))

    def stage(k, c2):
        return ad.at[k, c2, :, pl.ds(0, half)]

    def place(ex, dst, r0, nr, nc):
        rio = lax.broadcasted_iota(jnp.int32, (nr, nc), 0) + r0
        hot = rio.astype(F32) == slotcol[ex, :, 0:nc]
        scale = jnp.sum(jnp.where(hot, rwcol[ex, :, 0:nc], 0.0), axis=1, keepdims=True)
        scale = jnp.where(c == 0, 1.0, scale)
        hot = hot.astype(F32).astype(BF)
        for n in range(4):
            v = jnp.dot(hot, gat[0:nc, n * xb_w : (n + 1) * xb_w], preferred_element_type=F32)
            dst[r0 : r0 + nr, n * xb_w : (n + 1) * xb_w] = (v * scale).astype(BF)

    def away(k):
        return jnp.where(k == 2, 3, jnp.where(k == 3, 2, k))

    def d_copy(k, c2):
        return at(
            stage(k, c2),
            xd.at[c, k],
            d_ss.at[k, c2],
            d_rs.at[c, k],
            (dp, ((y + 4 - away(k)) % 4) * 2 + c2, t),
        )

    def d_wait(m, k):
        at(xd.at[m, k], xd.at[m, k], d_ss.at[0, 0], d_rs.at[m, k], (1 - dp, e, t)).wait_recv()

    def d0_copy(p, m):
        r = pl.ds(*PLACED[p])
        return at(
            ad.at[0, 1 - c, r, pl.ds(0, half)], xd.at[m, 0, r], d0_ss.at[p], d0_rs.at[p], (dp, y * 2 + 1 - c, t)
        )

    def first(p):
        gathered(p)
        r0, nr = PLACED[p]
        nc = (p + 1) * 2 * GRP
        place(y * 2 + 1 - c, stage(0, 1 - c), r0, nr, nc)
        d0_copy(p, c).start()
        place(e, xd.at[c, 0], r0, nr, nc)

    other = (1 - dp, e, t)

    def z_copy(u, k, r0, nr, f):
        r = pl.ds(r0, nr)
        return at(zs.at[k % 2, f, :, r], zr.at[k, f, :, r], z_ss.at[u, f], z_rs.at[u, f], other)

    def x_copy(m, p):
        if p == 0:
            return pltpu.make_async_copy(xd.at[m, 3], xd_hbm.at[m, pl.ds(0, RC)], x_sem.at[m, p])
        return pltpu.make_async_copy(
            xd.at[m, 0, pl.ds(*LATE)], xd_hbm.at[m, pl.ds(RC, LATE[1])], x_sem.at[m, p]
        )

    def z_left(u):
        k, part = UNITS[u]
        loop(0, NF, lambda f: z_copy(u, k, *part, f).wait_send())

    def project(u):
        k, (r0, nr) = UNITS[u]
        s = k % 2

        def piece(f):
            for m in range(2):
                v = jnp.dot(xd[m, k, r0 : r0 + nr], w[m, f], preferred_element_type=F32)
                own[s, f, m, r0 : r0 + nr] = v
                zs[s, f, m, r0 : r0 + nr] = v.astype(BF)
            z_copy(u, k, r0, nr, f).start()

        loop(0, NF, piece)

    first(0)
    for m in range(2):
        for f in range(NF):
            w_copy(m, f).wait()
    d0_copy(0, 1 - c).wait_recv()
    project(0)
    first(1)
    d0_copy(1, 1 - c).wait_recv()
    project(1)

    def dispatch(i):
        k, c2 = i // 2, i % 2
        place(((y + 4 - away(k)) % 4) * 2 + c2, stage(k, c2), 0, RC, TOKC)
        d_copy(k, c2).start()

    loop(2, 8, dispatch)
    cols = pl.ds(pl.multiple_of(c * 2 * GRP, 2 * GRP), 2 * GRP)
    rio = lax.broadcasted_iota(jnp.int32, (8, PR, 2 * GRP), 1) + c * (2 * CAP)
    hot = jnp.where(rio.astype(F32) == slotcol[:, :, cols], 1.0, 0.0).reshape(8 * PR, 2 * GRP)
    unhot[...] = hot.T.astype(BF)

    def ad_copy(m, p, f):
        cols = pl.ds(pl.multiple_of(f * fc, fc), fc)
        if p == 0:
            src, dst = ad.at[3, m, :, cols], ad_hbm.at[m, pl.ds(0, RC), cols]
        else:
            src, dst = ad.at[0, m, pl.ds(*LATE), cols], ad_hbm.at[m, pl.ds(RC, LATE[1]), cols]
        return pltpu.make_async_copy(src, dst, o_sem.at[m, p, f])

    def c1_copy(v, k, r0, nr, j):
        xb = (x + j) % 4
        r = pl.ds(r0, nr)
        return at(
            c1s.at[xb, r], c1r.at[v % 2, x, r], c1_ss.at[v, j], c1_rs.at[v, x], (dp, e, zlo * 4 + xb)
        )

    def c2_copy(k, c2):
        dev = (dp, ((y + AWAY[k]) % 4) * 2 + c2, t)
        return at(c2s.at[k, c2], res.at[e], c2_ss.at[k, c2], c2_rs.at[e], dev)

    def g_copy(m, i):
        dst = gu_hbm if m == 0 else gd_hbm
        rows = pl.ds(pl.multiple_of((i // NG) * xb_w, xb_w), xb_w)
        cols = pl.ds(pl.multiple_of((i % NG) * gc, gc), gc)
        return pltpu.make_async_copy(gs.at[i % 2], dst.at[rows, cols], g_sem.at[m, i % 2])

    def gradients(m, lo, hi):
        def band(n):
            rows = pl.ds(pl.multiple_of(n * xb_w, xb_w), xb_w)
            turned[...] = xd[m, 0:3, :, rows].reshape(3 * RC, xb_w).T
            turned[:, LATE[0] : RC] = jnp.zeros((xb_w, LATE[1]), BF)

            def tile(f):
                i = n * NG + f

                @pl.when(i >= 2)
                def _():
                    g_copy(m, i - 2).wait()

                if m == 1:

                    @pl.when(i < 2)
                    def _():
                        g_copy(0, i + 4 * NG - 2).wait()

                cols = pl.ds(pl.multiple_of(f * gc, gc), gc)
                right = ad[0:3, 1 - m, :, cols].reshape(3 * RC, gc)
                v = jnp.dot(turned[...], right, preferred_element_type=F32)
                gs[i % 2] = v.astype(BF)
                g_copy(m, i).start()

            loop(0, NG, tile)

        loop(lo, hi, band)

    def absorb(u):
        k, (r0, nr) = UNITS[u]
        s = k % 2
        r = slice(r0, r0 + nr)
        ar = slice(RC, RC + nr) if u == 5 else r
        acc[:, ar] = jnp.zeros((4, nr, xb_w), F32)

        def piece(f):
            z_copy(u, k, r0, nr, f).wait_recv()
            up = own[s, f, 0, r] + zr[k, f, 0, r].astype(F32)
            da = own[s, f, 1, r] + zr[k, f, 1, r].astype(F32)
            sg = jax.nn.sigmoid(up)
            cols = pl.ds(pl.multiple_of(f * fc, fc), fc)
            ad[k, 0, r, cols] = (up * sg).astype(BF)
            du = (da * sg * (1.0 + up * (1.0 - sg))).astype(BF)
            ad[k, 1, r, cols] = du
            if u >= 4:
                ad_copy(0, u - 4, f).start()
                ad_copy(1, u - 4, f).start()
            for n in range(4):
                acc[n, ar] += lax.dot_general(
                    du,
                    w[0, f, n * xb_w : (n + 1) * xb_w, :],
                    (((1,), (1,)), ((), ())),
                    preferred_element_type=F32,
                )

        loop(0, NF, piece)

    def c1_left(v):
        k, part = SUMS[v]
        loop(1, 4, lambda j: c1_copy(v, k, *part, j).wait_send())

    def spread(v):
        k, (r0, nr) = SUMS[v]
        if 0 < v < 4:
            c1_left(v - 1)

        def send(j):
            xb = (x + j) % 4
            c1s[xb, r0 : r0 + nr] = acc[xb, r0 : r0 + nr].astype(BF)
            c1_copy(v, k, r0, nr, j).start()

        loop(1, 4, send)

    def collect(v):
        k, (r0, nr) = SUMS[v]
        total = acc[x, r0 : r0 + nr]
        for j in range(1, 4):
            xs = (x + j) % 4
            r = c1r.at[v % 2, xs, pl.ds(r0, nr)]
            at(r, r, c1_ss.at[0, 0], c1_rs.at[v, xs], other).wait_recv()
            total += c1r[v % 2, xs, r0 : r0 + nr].astype(F32)
        return total

    def give_back(k, c2, part):
        part = jnp.concatenate([part, jnp.zeros((PR - 2 * CAP, xb_w), F32)], axis=0).astype(BF)
        if k > 0:
            c2s[k, c2] = part
            c2_copy(k, c2).start()
        else:

            @pl.when(c == c2)
            def _():
                res[e] = part

            @pl.when(c != c2)
            def _():
                c2s[k, c2] = part
                c2_copy(k, c2).start()

    for k in range(4):
        if k < 3:
            d_wait(0, k + 1)
            d_wait(1, k + 1)
            if k == 1:
                z_left(0)
                z_left(1)
            if k == 2:
                z_left(2)
            project(k + 2)
        else:
            for m in range(2):
                for p in range(2):
                    x_copy(m, p).start()
            z_left(3)
            project(5)
        if k == 0:
            d0_copy(0, c).wait_send()
            d0_copy(1, c).wait_send()
            absorb(0)
            absorb(1)
        else:
            d_copy(k, 0).wait_send()
            d_copy(k, 1).wait_send()
            absorb(k + 1)
        spread(k)
        if k == 2:
            ad[0, :, LATE[0] :] = jnp.zeros((2, LATE[1], NF * fc), BF)
            gradients(0, 0, 4)
            gradients(1, 0, 2)
        if k == 3:
            absorb(5)
            spread(4)
            gradients(1, 2, 3)
        total = collect(k)
        give_back(k, 0, total[0 : 2 * CAP])
        if k == 0:
            held[...] = total[2 * CAP :]
        else:
            give_back(k, 1, total[2 * CAP :])

    give_back(0, 1, jnp.concatenate([held[...], collect(4)], axis=0))

    def res_wait(j):
        i = (e + j) % 8
        at(res.at[i], res.at[i], c2_ss.at[0, 0], c2_rs.at[i], other).wait_recv()

    loop(1, 8, res_wait)
    back = res[...].reshape(8 * PR, xb_w)
    fin_s[...] = jnp.dot(unhot[...], back, preferred_element_type=F32).astype(BF)

    spot = (dp * 4 + x) * 2 + zlo

    def f_copy(j):
        i = (me16 + j) % 16
        row = pl.multiple_of(i * 16, 16)
        return at(fin_s.at[pl.ds(row, 16), :], fin_r.at[spot], f_ss.at[j], f_rs.at[spot], (i // 8, e, i % 8))

    loop(1, 16, lambda j: f_copy(j).start())
    fin_r[spot] = fin_s[pl.ds(pl.multiple_of(me16 * 16, 16), 16), :]

    gradients(1, 3, 4)

    def f_wait(j):
        i = (spot + j) % 16
        at(fin_r.at[i], fin_r.at[i], f_ss.at[0], f_rs.at[i], other).wait_recv()

    loop(1, 16, f_wait)
    for b in range(8):
        v = fin_r[b * 2].astype(F32) + fin_r[b * 2 + 1].astype(F32)
        out[:, b * xb_w : (b + 1) * xb_w] = v.astype(BF)

    for j in range(3):
        met_copy(j).wait_send()
    tok_copy(1).wait_send()
    loop(1, 4, lambda j: cot_copy(j).wait_send())

    @pl.when(c == 1)
    def _():
        tok_copy(0).wait_send()
        loop(0, 24, lambda i: fwd_copy(i // 3, 1 + i % 3).wait_send())

    @pl.when(c == 0)
    def _():
        cot_copy(0).wait_send()


    z_left(4)
    z_left(5)
    c1_left(3)
    c1_left(4)
    c2_copy(0, 1 - c).wait_send()
    for k in range(1, 4):
        for c2 in range(2):
            c2_copy(k, c2).wait_send()
    loop(1, 16, lambda j: f_copy(j).wait_send())
    for m in range(2):
        for f in range(NF):
            ad_copy(m, 0, f).wait()
            ad_copy(m, 1, f).wait()
        x_copy(m, 0).wait()
        x_copy(m, 1).wait()
    g_copy(1, 4 * NG - 2).wait()
    g_copy(1, 4 * NG - 1).wait()


def finish(up_part, down_part, xd, ad, gu, gd):
    for m, (part, dst) in enumerate(((up_part, gu), (down_part, gd))):
        last = lax.dot_general(
            xd[m], ad[1 - m], (((0,), (0,)), ((), ())), preferred_element_type=F32
        )
        dst[...] = (part[...].astype(F32) + last).astype(BF)


def shards(tokens, cotangent, expert_ids, route_weight, w_up, w_down):
    half, ff = w_up.shape[1], w_up.shape[2]
    rows = 4 * RC
    fc = ff // NF
    xb_w = half // 4
    vmem = pl.BlockSpec(memory_space=pltpu.VMEM)
    hbm = pl.BlockSpec(memory_space=pl.ANY)
    dma = pltpu.SemaphoreType.DMA
    grad = jax.ShapeDtypeStruct((half, ff), BF)
    out, xd, ad, gu, gd = pl.pallas_call(
        kernel,
        out_shape=(
            jax.ShapeDtypeStruct(cotangent.shape, BF),
            jax.ShapeDtypeStruct((2, FIN, half), BF),
            jax.ShapeDtypeStruct((2, FIN, ff), BF),
            grad,
            grad,
        ),
        in_specs=[vmem] * 4 + [hbm] * 2,
        out_specs=(vmem, hbm, hbm, hbm, hbm),
        scratch_shapes=[
            pltpu.VMEM((2, NF, half, fc), BF),
            pltpu.VMEM((TOKC, half), BF),
            pltpu.VMEM((4, 4, GRP), F32),
            pltpu.VMEM((8, 1, TOKC), F32),
            pltpu.VMEM((8, 1, TOKC), F32),
            pltpu.VMEM((2, 4, RC, half), BF),
            pltpu.VMEM((2, NF, 2, RC, fc), F32),
            pltpu.VMEM((2, NF, 2, RC, fc), BF),
            pltpu.VMEM((4, NF, 2, RC, fc), BF),
            pltpu.VMEM((4, 2, RC, ff), BF),
            pltpu.VMEM((4, FIN, xb_w), F32),
            pltpu.VMEM((4, FIN, xb_w), BF),
            pltpu.VMEM((2, 4, FIN, xb_w), BF),
            pltpu.VMEM((4, 2, PR, xb_w), BF),
            pltpu.VMEM((8, PR, xb_w), BF),
            pltpu.VMEM((2 * GRP, xb_w), BF),
            pltpu.VMEM((16, 16, xb_w), BF),
            pltpu.VMEM((2 * GRP, 8 * PR), BF),
            pltpu.VMEM((EARLY[1] - 2 * CAP, xb_w), F32),
            pltpu.VMEM((xb_w, 3 * RC), BF),
            pltpu.VMEM((2, xb_w, ff // NG), BF),
            dma((2, NF)),
            dma((4,)),
            dma((8, 3)),
            dma((32,)),
            dma((2,)),
            dma((4,)),
            dma((3,)),
            dma((4,)),
            dma((2,)),
            dma((2,)),
            dma((4, 2)),
            dma((2, 4)),
            dma((6, NF)),
            dma((6, NF)),
            dma((5, 4)),
            dma((5, 4)),
            dma((4, 2)),
            dma((8,)),
            dma((16,)),
            dma((16,)),
            dma((2, 2, NF)),
            dma((2, 2)),
            dma((2, 2)),
        ],
        compiler_params=pltpu.CompilerParams(
            collective_id=0, has_side_effects=True, vmem_limit_bytes=int(38.75 * 2**20)
        ),
        cost_estimate=pl.CostEstimate(
            flops=6 * rows * half * ff, bytes_accessed=4 * half * ff, transcendentals=rows * ff
        ),
    )(tokens, cotangent, expert_ids.T, route_weight.T, w_up, w_down)

    gb = 256
    gu, gd = pl.pallas_call(
        finish,
        grid=(half // gb,),
        out_shape=(grad, grad),
        in_specs=[
            pl.BlockSpec((gb, ff), lambda i: (i, 0)),
            pl.BlockSpec((gb, ff), lambda i: (i, 0)),
            pl.BlockSpec((2, FIN, gb), lambda i: (0, 0, i)),
            pl.BlockSpec((2, FIN, ff), lambda i: (0, 0, 0)),
        ],
        out_specs=(pl.BlockSpec((gb, ff), lambda i: (i, 0)),) * 2,
        compiler_params=pltpu.CompilerParams(vmem_limit_bytes=24 * 2**20),
    )(gu, gd, xd, ad)
    return out, gu[None], gd[None]


def solution(mesh):
    placed = (
        P(("dp", "expert"), None),
        P(("dp", "expert", "tensor"), None),
        P(("dp", "expert"), None),
        P(("dp", "expert"), None),
        P("expert", "dp", "tensor"),
        P("expert", "dp", "tensor"),
    )
    return jax.shard_map(
        shards,
        mesh=mesh,
        in_specs=placed,
        out_specs=(
            P(("dp", "expert", "tensor"), None),
            P("expert", "dp", "tensor"),
            P("expert", "dp", "tensor"),
        ),
        check_vma=False,
    )
```

```python
import jax
import jax.numpy as jnp
from jax import lax
from jax.experimental import pallas as pl
from jax.experimental.pallas import tpu as pltpu
from jax.sharding import PartitionSpec as P

CAP = 36
GRP = 128
RC = 4 * CAP
TOKC = 4 * GRP
PR = 80
NG = 4
NF = 4
WHOLE = (0, RC)
PLACED = ((0, 64), (64, 80))
EARLY = (0, 128)
LATE = (128, 16)
FIN = RC + LATE[1]
UNITS = ((0, (0, 64)), (0, (64, 64)), (1, WHOLE), (2, WHOLE), (3, WHOLE), (0, LATE))
SUMS = ((0, EARLY), (1, WHOLE), (2, WHOLE), (3, WHOLE), (0, (RC, LATE[1])))
AWAY = (0, 1, 3, 2)
MESH = pl.DeviceIdType.MESH
BF = jnp.bfloat16
F32 = jnp.float32


def kernel(
    tok,
    cot,
    ids,
    rw,
    wu_hbm,
    wd_hbm,
    out,
    xd_hbm,
    ad_hbm,
    gu_hbm,
    gd_hbm,
    w,
    gat,
    metas,
    slotcol,
    rwcol,
    xd,
    own,
    zs,
    zr,
    ad,
    acc,
    c1s,
    c1r,
    c2s,
    res,
    fin_s,
    fin_r,
    unhot,
    held,
    turned,
    gs,
    w_sem,
    cot_ss,
    fwd_ss,
    cot_rs,
    tok_ss,
    tok_rs,
    met_ss,
    met_rs,
    d0_ss,
    d0_rs,
    d_ss,
    d_rs,
    z_ss,
    z_rs,
    c1_ss,
    c1_rs,
    c2_ss,
    c2_rs,
    f_ss,
    f_rs,
    o_sem,
    x_sem,
    g_sem,
):
    dp, e, t = lax.axis_index("dp"), lax.axis_index("expert"), lax.axis_index("tensor")
    y, c = e // 2, e % 2
    zlo, x = t // 4, t % 4
    z = dp * 2 + zlo
    half = w.shape[2]
    fc = w.shape[3]
    xb_w = half // 4
    gc = NF * fc // NG

    def at(src, dst, ss, rs, dev):
        return pltpu.make_async_remote_copy(
            src_ref=src, dst_ref=dst, send_sem=ss, recv_sem=rs, device_id=dev, device_id_type=MESH
        )

    def loop(lo, hi, fn):
        def step(i, carry):
            fn(i)
            return carry

        lax.fori_loop(lo, hi, step, 0)

    def w_copy(m, f):
        src = wu_hbm if m == 0 else wd_hbm
        return pltpu.make_async_copy(
            src.at[0, :, pl.ds(pl.multiple_of(f * fc, fc), fc)], w.at[m, f], w_sem.at[m, f]
        )

    for m in range(2):
        for f in range(NF):
            w_copy(m, f).start()

    barrier = pltpu.get_barrier_semaphore()
    me16 = dp * 8 + t

    def greet(d, ex, tt):
        pl.semaphore_signal(barrier, inc=1, device_id=(d, ex, tt), device_id_type=MESH)

    def greet_plane(j):
        i = (me16 + j) % 16
        greet(i // 8, e, i % 8)

    loop(1, 16, greet_plane)
    for j in range(4):
        zz = (z + j) % 4
        greet(zz // 2, y * 2 + 1 - c, (zz % 2) * 4 + x)
    for j in range(1, 4):
        for c2 in range(2):
            greet(dp, ((y + j) % 4) * 2 + c2, t)
    mine = c * 2 + dp
    metas[mine, 0:2, :] = ids[...].astype(F32)
    metas[mine, 2:4, :] = rw[...]
    pl.semaphore_wait(barrier, 25)

    tn = (1 - zlo) * 4 + x

    def met_copy(j):
        dev = ((dp, y * 2 + 1 - c, t), (1 - dp, y * 2 + c, tn), (1 - dp, y * 2 + 1 - c, tn))[j]
        return at(metas.at[mine], metas.at[mine], met_ss.at[j], met_rs.at[mine], dev)

    for j in range(3):
        met_copy(j).start()

    grow = pl.multiple_of(mine * GRP, GRP)
    trow = pl.multiple_of(mine * GRP + t * 16, 16)

    def tok_copy(j):
        h = dp if j == 0 else 1 - dp
        dev = (dp, y * 2, t) if j == 0 else (1 - dp, y * 2, tn)
        return at(
            tok.at[:, pl.ds(pl.multiple_of(h * half, half), half)],
            gat.at[pl.ds(grow, GRP), :],
            tok_ss.at[j],
            tok_rs.at[mine],
            dev,
        )

    sidx = mine * 8 + t

    def cot_copy(j):
        zz = (z + j) % 4
        return at(
            cot.at[:, pl.ds(pl.multiple_of((zz // 2) * half, half), half)],
            gat.at[pl.ds(trow, 16), :],
            cot_ss.at[j],
            cot_rs.at[sidx],
            (zz // 2, y * 2 + 1, (zz % 2) * 4 + x),
        )

    def shard(q, xs):
        zz = (z + q) % 4
        return ((q // 4) * 2 + zz // 2) * 8 + (zz % 2) * 4 + xs

    def rows_of(i):
        return gat.at[pl.ds(pl.multiple_of(i * 16, 16), 16), :]

    def fwd_copy(q, j):
        i = shard(q, x)
        return at(
            rows_of(i), rows_of(i), fwd_ss.at[q, j - 1], cot_rs.at[i], (dp, e, zlo * 4 + (x + j) % 4)
        )

    def cot_wait(i):
        at(rows_of(i), rows_of(i), cot_ss.at[0], cot_rs.at[i], (1 - dp, e, tn)).wait_recv()

    for j in range(1, 4):
        cot_copy(j).start()

    @pl.when(c == 0)
    def _():
        cot_copy(0).start()
        tok_copy(1).start()
        gat[pl.ds(grow, GRP), :] = tok[:, pl.ds(pl.multiple_of(dp * half, half), half)]

    @pl.when(c == 1)
    def _():
        gat[pl.ds(trow, 16), :] = cot[:, pl.ds(pl.multiple_of(dp * half, half), half)]

        def forward(q):
            @pl.when(q != 4)
            def _():
                cot_wait(shard(q, x))

            for j in range(1, 4):
                fwd_copy(q, j).start()

        loop(0, 8, forward)
        tok_copy(1).start()
        tok_copy(0).start()

    def met_wait(j):
        g = (mine + j) % 4
        at(metas.at[g], metas.at[g], met_ss.at[0], met_rs.at[g], (dp, y * 2 + 1 - c, t)).wait_recv()

    loop(1, 4, met_wait)
    eio = lax.broadcasted_iota(jnp.int32, (8, GRP), 0).astype(F32)
    tri = (
        lax.broadcasted_iota(jnp.int32, (GRP, GRP), 0) < lax.broadcasted_iota(jnp.int32, (GRP, GRP), 1)
    ).astype(F32).astype(BF)
    for g in range(4):
        mg = metas[g]
        h0 = mg[0:1, :] == eio
        h1 = mg[1:2, :] == eio
        hot = jnp.where(h0, 1.0, jnp.where(h1, 1.0, 0.0))
        slot = jnp.dot(hot.astype(BF), tri, preferred_element_type=F32)
        sc = jnp.where(hot > 0.5, slot + float(g * CAP), -1.0)
        rc = jnp.where(h0, mg[2:3, :], jnp.where(h1, mg[3:4, :], 0.0))
        for k in range(8):
            slotcol[k, 0:1, g * GRP : (g + 1) * GRP] = sc[k : k + 1, :]
            rwcol[k, 0:1, g * GRP : (g + 1) * GRP] = rc[k : k + 1, :]

    def tok_wait(g):
        group = gat.at[pl.ds(pl.multiple_of(g * GRP, GRP), GRP), :]
        at(group, group, tok_ss.at[0], tok_rs.at[g], (1 - dp, e, tn)).wait_recv()

    def gathered(c2):
        @pl.when(c == 0)
        def _():
            if c2 == 0:
                tok_wait(1 - dp)
            else:
                tok_wait(2)
                tok_wait(3)

        @pl.when(c == 1)
        def _():
            loop(0, 12, lambda i: cot_wait(shard(c2 * 4 + i % 4, (x + 1 + i // 4) % 4)))

    def stage(k, c2):
        return ad.at[k, c2, :, pl.ds(0, half)]

    def place(ex, dst, r0, nr, nc):
        rio = lax.broadcasted_iota(jnp.int32, (nr, nc), 0) + r0
        hot = rio.astype(F32) == slotcol[ex, :, 0:nc]
        scale = jnp.sum(jnp.where(hot, rwcol[ex, :, 0:nc], 0.0), axis=1, keepdims=True)
        scale = jnp.where(c == 0, 1.0, scale)
        hot = hot.astype(F32).astype(BF)
        for n in range(4):
            v = jnp.dot(hot, gat[0:nc, n * xb_w : (n + 1) * xb_w], preferred_element_type=F32)
            dst[r0 : r0 + nr, n * xb_w : (n + 1) * xb_w] = (v * scale).astype(BF)

    def away(k):
        return jnp.where(k == 2, 3, jnp.where(k == 3, 2, k))

    def d_copy(k, c2):
        return at(
            stage(k, c2),
            xd.at[c, k],
            d_ss.at[k, c2],
            d_rs.at[c, k],
            (dp, ((y + 4 - away(k)) % 4) * 2 + c2, t),
        )

    def d_wait(m, k):
        at(xd.at[m, k], xd.at[m, k], d_ss.at[0, 0], d_rs.at[m, k], (1 - dp, e, t)).wait_recv()

    def d0_copy(p, m):
        r = pl.ds(*PLACED[p])
        return at(
            ad.at[0, 1 - c, r, pl.ds(0, half)], xd.at[m, 0, r], d0_ss.at[p], d0_rs.at[p], (dp, y * 2 + 1 - c, t)
        )

    def first(p):
        gathered(p)
        r0, nr = PLACED[p]
        nc = (p + 1) * 2 * GRP
        place(y * 2 + 1 - c, stage(0, 1 - c), r0, nr, nc)
        d0_copy(p, c).start()
        place(e, xd.at[c, 0], r0, nr, nc)

    other = (1 - dp, e, t)

    def z_copy(u, k, r0, nr, f):
        r = pl.ds(r0, nr)
        return at(zs.at[k % 2, f, :, r], zr.at[k, f, :, r], z_ss.at[u, f], z_rs.at[u, f], other)

    def x_copy(m, p):
        if p == 0:
            return pltpu.make_async_copy(xd.at[m, 3], xd_hbm.at[m, pl.ds(0, RC)], x_sem.at[m, p])
        return pltpu.make_async_copy(
            xd.at[m, 0, pl.ds(*LATE)], xd_hbm.at[m, pl.ds(RC, LATE[1])], x_sem.at[m, p]
        )

    def z_left(u):
        k, part = UNITS[u]
        loop(0, NF, lambda f: z_copy(u, k, *part, f).wait_send())

    def project(u):
        k, (r0, nr) = UNITS[u]
        s = k % 2

        def piece(f):
            for m in range(2):
                v = jnp.dot(xd[m, k, r0 : r0 + nr], w[m, f], preferred_element_type=F32)
                own[s, f, m, r0 : r0 + nr] = v
                zs[s, f, m, r0 : r0 + nr] = v.astype(BF)
            z_copy(u, k, r0, nr, f).start()

        loop(0, NF, piece)

    first(0)
    for m in range(2):
        for f in range(NF):
            w_copy(m, f).wait()
    d0_copy(0, 1 - c).wait_recv()
    project(0)
    first(1)
    d0_copy(1, 1 - c).wait_recv()
    project(1)

    def dispatch(i):
        k, c2 = i // 2, i % 2
        place(((y + 4 - away(k)) % 4) * 2 + c2, stage(k, c2), 0, RC, TOKC)
        d_copy(k, c2).start()

    loop(2, 8, dispatch)
    cols = pl.ds(pl.multiple_of(c * 2 * GRP, 2 * GRP), 2 * GRP)
    rio = lax.broadcasted_iota(jnp.int32, (8, PR, 2 * GRP), 1) + c * (2 * CAP)
    hot = jnp.where(rio.astype(F32) == slotcol[:, :, cols], 1.0, 0.0).reshape(8 * PR, 2 * GRP)
    unhot[...] = hot.T.astype(BF)

    def ad_copy(m, p, f):
        cols = pl.ds(pl.multiple_of(f * fc, fc), fc)
        if p == 0:
            src, dst = ad.at[3, m, :, cols], ad_hbm.at[m, pl.ds(0, RC), cols]
        else:
            src, dst = ad.at[0, m, pl.ds(*LATE), cols], ad_hbm.at[m, pl.ds(RC, LATE[1]), cols]
        return pltpu.make_async_copy(src, dst, o_sem.at[m, p, f])

    def c1_copy(v, k, r0, nr, j):
        xb = (x + j) % 4
        r = pl.ds(r0, nr)
        return at(
            c1s.at[xb, r], c1r.at[v % 2, x, r], c1_ss.at[v, j], c1_rs.at[v, x], (dp, e, zlo * 4 + xb)
        )

    def c2_copy(k, c2):
        dev = (dp, ((y + AWAY[k]) % 4) * 2 + c2, t)
        return at(c2s.at[k, c2], res.at[e], c2_ss.at[k, c2], c2_rs.at[e], dev)

    def g_copy(m, i):
        dst = gu_hbm if m == 0 else gd_hbm
        rows = pl.ds(pl.multiple_of((i // NG) * xb_w, xb_w), xb_w)
        cols = pl.ds(pl.multiple_of((i % NG) * gc, gc), gc)
        return pltpu.make_async_copy(gs.at[i % 2], dst.at[rows, cols], g_sem.at[m, i % 2])

    def gradients(m, lo, hi):
        def band(n):
            rows = pl.ds(pl.multiple_of(n * xb_w, xb_w), xb_w)
            turned[...] = xd[m, 0:3, :, rows].reshape(3 * RC, xb_w).T
            turned[:, LATE[0] : RC] = jnp.zeros((xb_w, LATE[1]), BF)

            def tile(f):
                i = n * NG + f

                @pl.when(i >= 2)
                def _():
                    g_copy(m, i - 2).wait()

                if m == 1:

                    @pl.when(i < 2)
                    def _():
                        g_copy(0, i + 4 * NG - 2).wait()

                cols = pl.ds(pl.multiple_of(f * gc, gc), gc)
                right = ad[0:3, 1 - m, :, cols].reshape(3 * RC, gc)
                v = jnp.dot(turned[...], right, preferred_element_type=F32)
                gs[i % 2] = v.astype(BF)
                g_copy(m, i).start()

            loop(0, NG, tile)

        loop(lo, hi, band)

    def absorb(u):
        k, (r0, nr) = UNITS[u]
        s = k % 2
        r = slice(r0, r0 + nr)
        ar = slice(RC, RC + nr) if u == 5 else r
        acc[:, ar] = jnp.zeros((4, nr, xb_w), F32)

        def piece(f):
            z_copy(u, k, r0, nr, f).wait_recv()
            up = own[s, f, 0, r] + zr[k, f, 0, r].astype(F32)
            da = own[s, f, 1, r] + zr[k, f, 1, r].astype(F32)
            sg = jax.nn.sigmoid(up)
            cols = pl.ds(pl.multiple_of(f * fc, fc), fc)
            ad[k, 0, r, cols] = (up * sg).astype(BF)
            du = (da * sg * (1.0 + up * (1.0 - sg))).astype(BF)
            ad[k, 1, r, cols] = du
            if u >= 4:
                ad_copy(0, u - 4, f).start()
                ad_copy(1, u - 4, f).start()
            for n in range(4):
                acc[n, ar] += lax.dot_general(
                    du,
                    w[0, f, n * xb_w : (n + 1) * xb_w, :],
                    (((1,), (1,)), ((), ())),
                    preferred_element_type=F32,
                )

        loop(0, NF, piece)

    def c1_left(v):
        k, part = SUMS[v]
        loop(1, 4, lambda j: c1_copy(v, k, *part, j).wait_send())

    def spread(v):
        k, (r0, nr) = SUMS[v]
        if 0 < v < 4:
            c1_left(v - 1)

        def send(j):
            xb = (x + j) % 4
            c1s[xb, r0 : r0 + nr] = acc[xb, r0 : r0 + nr].astype(BF)
            c1_copy(v, k, r0, nr, j).start()

        loop(1, 4, send)

    def collect(v):
        k, (r0, nr) = SUMS[v]
        total = acc[x, r0 : r0 + nr]
        for j in range(1, 4):
            xs = (x + j) % 4
            r = c1r.at[v % 2, xs, pl.ds(r0, nr)]
            at(r, r, c1_ss.at[0, 0], c1_rs.at[v, xs], other).wait_recv()
            total += c1r[v % 2, xs, r0 : r0 + nr].astype(F32)
        return total

    def give_back(k, c2, part):
        part = jnp.concatenate([part, jnp.zeros((PR - 2 * CAP, xb_w), F32)], axis=0).astype(BF)
        if k > 0:
            c2s[k, c2] = part
            c2_copy(k, c2).start()
        else:

            @pl.when(c == c2)
            def _():
                res[e] = part

            @pl.when(c != c2)
            def _():
                c2s[k, c2] = part
                c2_copy(k, c2).start()

    for k in range(4):
        if k < 3:
            d_wait(0, k + 1)
            d_wait(1, k + 1)
            if k == 1:
                z_left(0)
                z_left(1)
            if k == 2:
                z_left(2)
            project(k + 2)
        else:
            for m in range(2):
                for p in range(2):
                    x_copy(m, p).start()
            z_left(3)
            project(5)
        if k == 0:
            d0_copy(0, c).wait_send()
            d0_copy(1, c).wait_send()
            absorb(0)
            absorb(1)
        else:
            d_copy(k, 0).wait_send()
            d_copy(k, 1).wait_send()
            absorb(k + 1)
        spread(k)
        if k == 2:
            ad[0, :, LATE[0] :] = jnp.zeros((2, LATE[1], NF * fc), BF)
            gradients(0, 0, 4)
            gradients(1, 0, 1)
        if k == 3:
            absorb(5)
            spread(4)
            gradients(1, 1, 2)
        total = collect(k)
        give_back(k, 0, total[0 : 2 * CAP])
        if k == 0:
            held[...] = total[2 * CAP :]
        else:
            give_back(k, 1, total[2 * CAP :])

    give_back(0, 1, jnp.concatenate([held[...], collect(4)], axis=0))
    gradients(1, 2, 3)

    def res_wait(j):
        i = (e + j) % 8
        at(res.at[i], res.at[i], c2_ss.at[0, 0], c2_rs.at[i], other).wait_recv()

    loop(1, 8, res_wait)
    back = res[...].reshape(8 * PR, xb_w)
    fin_s[...] = jnp.dot(unhot[...], back, preferred_element_type=F32).astype(BF)

    spot = (dp * 4 + x) * 2 + zlo

    def f_copy(j):
        i = (me16 + j) % 16
        row = pl.multiple_of(i * 16, 16)
        return at(fin_s.at[pl.ds(row, 16), :], fin_r.at[spot], f_ss.at[j], f_rs.at[spot], (i // 8, e, i % 8))

    loop(1, 16, lambda j: f_copy(j).start())
    fin_r[spot] = fin_s[pl.ds(pl.multiple_of(me16 * 16, 16), 16), :]

    gradients(1, 3, 4)

    def f_wait(j):
        i = (spot + j) % 16
        at(fin_r.at[i], fin_r.at[i], f_ss.at[0], f_rs.at[i], other).wait_recv()

    loop(1, 16, f_wait)
    for b in range(8):
        v = fin_r[b * 2].astype(F32) + fin_r[b * 2 + 1].astype(F32)
        out[:, b * xb_w : (b + 1) * xb_w] = v.astype(BF)

    for j in range(3):
        met_copy(j).wait_send()
    tok_copy(1).wait_send()
    loop(1, 4, lambda j: cot_copy(j).wait_send())

    @pl.when(c == 1)
    def _():
        tok_copy(0).wait_send()
        loop(0, 24, lambda i: fwd_copy(i // 3, 1 + i % 3).wait_send())

    @pl.when(c == 0)
    def _():
        cot_copy(0).wait_send()


    z_left(4)
    z_left(5)
    c1_left(3)
    c1_left(4)
    c2_copy(0, 1 - c).wait_send()
    for k in range(1, 4):
        for c2 in range(2):
            c2_copy(k, c2).wait_send()
    loop(1, 16, lambda j: f_copy(j).wait_send())
    for m in range(2):
        for f in range(NF):
            ad_copy(m, 0, f).wait()
            ad_copy(m, 1, f).wait()
        x_copy(m, 0).wait()
        x_copy(m, 1).wait()
    g_copy(1, 4 * NG - 2).wait()
    g_copy(1, 4 * NG - 1).wait()


def finish(up_part, down_part, xd, ad, gu, gd):
    for m, (part, dst) in enumerate(((up_part, gu), (down_part, gd))):
        last = lax.dot_general(
            xd[m], ad[1 - m], (((0,), (0,)), ((), ())), preferred_element_type=F32
        )
        dst[...] = (part[...].astype(F32) + last).astype(BF)


def shards(tokens, cotangent, expert_ids, route_weight, w_up, w_down):
    half, ff = w_up.shape[1], w_up.shape[2]
    rows = 4 * RC
    fc = ff // NF
    xb_w = half // 4
    vmem = pl.BlockSpec(memory_space=pltpu.VMEM)
    hbm = pl.BlockSpec(memory_space=pl.ANY)
    dma = pltpu.SemaphoreType.DMA
    grad = jax.ShapeDtypeStruct((half, ff), BF)
    out, xd, ad, gu, gd = pl.pallas_call(
        kernel,
        out_shape=(
            jax.ShapeDtypeStruct(cotangent.shape, BF),
            jax.ShapeDtypeStruct((2, FIN, half), BF),
            jax.ShapeDtypeStruct((2, FIN, ff), BF),
            grad,
            grad,
        ),
        in_specs=[vmem] * 4 + [hbm] * 2,
        out_specs=(vmem, hbm, hbm, hbm, hbm),
        scratch_shapes=[
            pltpu.VMEM((2, NF, half, fc), BF),
            pltpu.VMEM((TOKC, half), BF),
            pltpu.VMEM((4, 4, GRP), F32),
            pltpu.VMEM((8, 1, TOKC), F32),
            pltpu.VMEM((8, 1, TOKC), F32),
            pltpu.VMEM((2, 4, RC, half), BF),
            pltpu.VMEM((2, NF, 2, RC, fc), F32),
            pltpu.VMEM((2, NF, 2, RC, fc), BF),
            pltpu.VMEM((4, NF, 2, RC, fc), BF),
            pltpu.VMEM((4, 2, RC, ff), BF),
            pltpu.VMEM((4, FIN, xb_w), F32),
            pltpu.VMEM((4, FIN, xb_w), BF),
            pltpu.VMEM((2, 4, FIN, xb_w), BF),
            pltpu.VMEM((4, 2, PR, xb_w), BF),
            pltpu.VMEM((8, PR, xb_w), BF),
            pltpu.VMEM((2 * GRP, xb_w), BF),
            pltpu.VMEM((16, 16, xb_w), BF),
            pltpu.VMEM((2 * GRP, 8 * PR), BF),
            pltpu.VMEM((EARLY[1] - 2 * CAP, xb_w), F32),
            pltpu.VMEM((xb_w, 3 * RC), BF),
            pltpu.VMEM((2, xb_w, ff // NG), BF),
            dma((2, NF)),
            dma((4,)),
            dma((8, 3)),
            dma((32,)),
            dma((2,)),
            dma((4,)),
            dma((3,)),
            dma((4,)),
            dma((2,)),
            dma((2,)),
            dma((4, 2)),
            dma((2, 4)),
            dma((6, NF)),
            dma((6, NF)),
            dma((5, 4)),
            dma((5, 4)),
            dma((4, 2)),
            dma((8,)),
            dma((16,)),
            dma((16,)),
            dma((2, 2, NF)),
            dma((2, 2)),
            dma((2, 2)),
        ],
        compiler_params=pltpu.CompilerParams(
            collective_id=0, has_side_effects=True, vmem_limit_bytes=int(38.75 * 2**20)
        ),
        cost_estimate=pl.CostEstimate(
            flops=6 * rows * half * ff, bytes_accessed=4 * half * ff, transcendentals=rows * ff
        ),
    )(tokens, cotangent, expert_ids.T, route_weight.T, w_up, w_down)

    gb = 384
    gu, gd = pl.pallas_call(
        finish,
        grid=(half // gb,),
        out_shape=(grad, grad),
        in_specs=[
            pl.BlockSpec((gb, ff), lambda i: (i, 0)),
            pl.BlockSpec((gb, ff), lambda i: (i, 0)),
            pl.BlockSpec((2, FIN, gb), lambda i: (0, 0, i)),
            pl.BlockSpec((2, FIN, ff), lambda i: (0, 0, 0)),
        ],
        out_specs=(pl.BlockSpec((gb, ff), lambda i: (i, 0)),) * 2,
        compiler_params=pltpu.CompilerParams(vmem_limit_bytes=24 * 2**20),
    )(gu, gd, xd, ad)
    return out, gu[None], gd[None]


def solution(mesh):
    placed = (
        P(("dp", "expert"), None),
        P(("dp", "expert", "tensor"), None),
        P(("dp", "expert"), None),
        P(("dp", "expert"), None),
        P("expert", "dp", "tensor"),
        P("expert", "dp", "tensor"),
    )
    return jax.shard_map(
        shards,
        mesh=mesh,
        in_specs=placed,
        out_specs=(
            P(("dp", "expert", "tensor"), None),
            P("expert", "dp", "tensor"),
            P("expert", "dp", "tensor"),
        ),
        check_vma=False,
    )
```

```python
import jax
import jax.numpy as jnp
from jax import lax
from jax.experimental import pallas as pl
from jax.experimental.pallas import tpu as pltpu
from jax.sharding import PartitionSpec as P

CAP = 36
GRP = 128
RC = 4 * CAP
TOKC = 4 * GRP
PR = 80
NG = 4
NF = 4
WHOLE = (0, RC)
PLACED = ((0, 64), (64, 80))
EARLY = (0, 128)
LATE = (128, 16)
FIN = RC + LATE[1]
UNITS = ((0, (0, 64)), (0, (64, 64)), (1, WHOLE), (2, WHOLE), (3, WHOLE), (0, LATE))
SUMS = ((0, EARLY), (1, WHOLE), (2, WHOLE), (3, WHOLE), (0, (RC, LATE[1])))
AWAY = (0, 1, 3, 2)
MESH = pl.DeviceIdType.MESH
BF = jnp.bfloat16
F32 = jnp.float32


def kernel(
    tok,
    cot,
    ids,
    rw,
    wu_hbm,
    wd_hbm,
    out,
    xd_hbm,
    ad_hbm,
    gu_hbm,
    gd_hbm,
    w,
    gat,
    metas,
    slotcol,
    rwcol,
    xd,
    own,
    zs,
    zr,
    ad,
    acc,
    c1s,
    c1r,
    c2s,
    res,
    fin_s,
    fin_r,
    unhot,
    held,
    turned,
    gs,
    w_sem,
    cot_ss,
    fwd_ss,
    cot_rs,
    tok_ss,
    tok_rs,
    met_ss,
    met_rs,
    d0_ss,
    d0_rs,
    d_ss,
    d_rs,
    z_ss,
    z_rs,
    c1_ss,
    c1_rs,
    c2_ss,
    c2_rs,
    f_ss,
    f_rs,
    o_sem,
    x_sem,
    g_sem,
):
    dp, e, t = lax.axis_index("dp"), lax.axis_index("expert"), lax.axis_index("tensor")
    y, c = e // 2, e % 2
    zlo, x = t // 4, t % 4
    z = dp * 2 + zlo
    half = w.shape[2]
    fc = w.shape[3]
    xb_w = half // 4
    gc = NF * fc // NG

    def at(src, dst, ss, rs, dev):
        return pltpu.make_async_remote_copy(
            src_ref=src, dst_ref=dst, send_sem=ss, recv_sem=rs, device_id=dev, device_id_type=MESH
        )

    def loop(lo, hi, fn):
        def step(i, carry):
            fn(i)
            return carry

        lax.fori_loop(lo, hi, step, 0)

    def w_copy(m, f):
        src = wu_hbm if m == 0 else wd_hbm
        return pltpu.make_async_copy(
            src.at[0, :, pl.ds(pl.multiple_of(f * fc, fc), fc)], w.at[m, f], w_sem.at[m, f]
        )

    for m in range(2):
        for f in range(NF):
            w_copy(m, f).start()

    barrier = pltpu.get_barrier_semaphore()
    me16 = dp * 8 + t

    def greet(d, ex, tt):
        pl.semaphore_signal(barrier, inc=1, device_id=(d, ex, tt), device_id_type=MESH)

    def greet_plane(j):
        i = (me16 + j) % 16
        greet(i // 8, e, i % 8)

    loop(1, 16, greet_plane)
    for j in range(4):
        zz = (z + j) % 4
        greet(zz // 2, y * 2 + 1 - c, (zz % 2) * 4 + x)
    for j in range(1, 4):
        for c2 in range(2):
            greet(dp, ((y + j) % 4) * 2 + c2, t)
    mine = c * 2 + dp
    metas[mine, 0:2, :] = ids[...].astype(F32)
    metas[mine, 2:4, :] = rw[...]
    pl.semaphore_wait(barrier, 25)

    tn = (1 - zlo) * 4 + x

    def met_copy(j):
        dev = ((dp, y * 2 + 1 - c, t), (1 - dp, y * 2 + c, tn), (1 - dp, y * 2 + 1 - c, tn))[j]
        return at(metas.at[mine], metas.at[mine], met_ss.at[j], met_rs.at[mine], dev)

    for j in range(3):
        met_copy(j).start()

    grow = pl.multiple_of(mine * GRP, GRP)
    trow = pl.multiple_of(mine * GRP + t * 16, 16)

    def tok_copy(j):
        h = dp if j == 0 else 1 - dp
        dev = (dp, y * 2, t) if j == 0 else (1 - dp, y * 2, tn)
        return at(
            tok.at[:, pl.ds(pl.multiple_of(h * half, half), half)],
            gat.at[pl.ds(grow, GRP), :],
            tok_ss.at[j],
            tok_rs.at[mine],
            dev,
        )

    sidx = mine * 8 + t

    def cot_copy(j):
        zz = (z + j) % 4
        return at(
            cot.at[:, pl.ds(pl.multiple_of((zz // 2) * half, half), half)],
            gat.at[pl.ds(trow, 16), :],
            cot_ss.at[j],
            cot_rs.at[sidx],
            (zz // 2, y * 2 + 1, (zz % 2) * 4 + x),
        )

    def shard(q, xs):
        zz = (z + q) % 4
        return ((q // 4) * 2 + zz // 2) * 8 + (zz % 2) * 4 + xs

    def rows_of(i):
        return gat.at[pl.ds(pl.multiple_of(i * 16, 16), 16), :]

    def fwd_copy(q, j):
        i = shard(q, x)
        return at(
            rows_of(i), rows_of(i), fwd_ss.at[q, j - 1], cot_rs.at[i], (dp, e, zlo * 4 + (x + j) % 4)
        )

    def cot_wait(i):
        at(rows_of(i), rows_of(i), cot_ss.at[0], cot_rs.at[i], (1 - dp, e, tn)).wait_recv()

    for j in range(1, 4):
        cot_copy(j).start()

    @pl.when(c == 0)
    def _():
        cot_copy(0).start()
        tok_copy(1).start()
        gat[pl.ds(grow, GRP), :] = tok[:, pl.ds(pl.multiple_of(dp * half, half), half)]

    @pl.when(c == 1)
    def _():
        gat[pl.ds(trow, 16), :] = cot[:, pl.ds(pl.multiple_of(dp * half, half), half)]

        def forward(q):
            @pl.when(q != 4)
            def _():
                cot_wait(shard(q, x))

            for j in range(1, 4):
                fwd_copy(q, j).start()

        loop(0, 8, forward)
        tok_copy(1).start()
        tok_copy(0).start()

    def met_wait(j):
        g = (mine + j) % 4
        at(metas.at[g], metas.at[g], met_ss.at[0], met_rs.at[g], (dp, y * 2 + 1 - c, t)).wait_recv()

    loop(1, 4, met_wait)
    eio = lax.broadcasted_iota(jnp.int32, (8, GRP), 0).astype(F32)
    tri = (
        lax.broadcasted_iota(jnp.int32, (GRP, GRP), 0) < lax.broadcasted_iota(jnp.int32, (GRP, GRP), 1)
    ).astype(F32).astype(BF)
    for g in range(4):
        mg = metas[g]
        h0 = mg[0:1, :] == eio
        h1 = mg[1:2, :] == eio
        hot = jnp.where(h0, 1.0, jnp.where(h1, 1.0, 0.0))
        slot = jnp.dot(hot.astype(BF), tri, preferred_element_type=F32)
        sc = jnp.where(hot > 0.5, slot + float(g * CAP), -1.0)
        rc = jnp.where(h0, mg[2:3, :], jnp.where(h1, mg[3:4, :], 0.0))
        for k in range(8):
            slotcol[k, 0:1, g * GRP : (g + 1) * GRP] = sc[k : k + 1, :]
            rwcol[k, 0:1, g * GRP : (g + 1) * GRP] = rc[k : k + 1, :]

    def tok_wait(g):
        group = gat.at[pl.ds(pl.multiple_of(g * GRP, GRP), GRP), :]
        at(group, group, tok_ss.at[0], tok_rs.at[g], (1 - dp, e, tn)).wait_recv()

    def gathered(c2):
        @pl.when(c == 0)
        def _():
            if c2 == 0:
                tok_wait(1 - dp)
            else:
                tok_wait(2)
                tok_wait(3)

        @pl.when(c == 1)
        def _():
            loop(0, 12, lambda i: cot_wait(shard(c2 * 4 + i % 4, (x + 1 + i // 4) % 4)))

    def stage(k, c2):
        return ad.at[k, c2, :, pl.ds(0, half)]

    def place(ex, dst, r0, nr, nc):
        rio = lax.broadcasted_iota(jnp.int32, (nr, nc), 0) + r0
        hot = rio.astype(F32) == slotcol[ex, :, 0:nc]
        scale = jnp.sum(jnp.where(hot, rwcol[ex, :, 0:nc], 0.0), axis=1, keepdims=True)
        scale = jnp.where(c == 0, 1.0, scale)
        hot = hot.astype(F32).astype(BF)
        for n in range(4):
            v = jnp.dot(hot, gat[0:nc, n * xb_w : (n + 1) * xb_w], preferred_element_type=F32)
            dst[r0 : r0 + nr, n * xb_w : (n + 1) * xb_w] = (v * scale).astype(BF)

    def away(k):
        return jnp.where(k == 2, 3, jnp.where(k == 3, 2, k))

    def d_copy(k, c2):
        return at(
            stage(k, c2),
            xd.at[c, k],
            d_ss.at[k, c2],
            d_rs.at[c, k],
            (dp, ((y + 4 - away(k)) % 4) * 2 + c2, t),
        )

    def d_wait(m, k):
        at(xd.at[m, k], xd.at[m, k], d_ss.at[0, 0], d_rs.at[m, k], (1 - dp, e, t)).wait_recv()

    def d0_copy(p, m):
        r = pl.ds(*PLACED[p])
        return at(
            ad.at[0, 1 - c, r, pl.ds(0, half)], xd.at[m, 0, r], d0_ss.at[p], d0_rs.at[p], (dp, y * 2 + 1 - c, t)
        )

    def first(p):
        gathered(p)
        r0, nr = PLACED[p]
        nc = (p + 1) * 2 * GRP
        place(y * 2 + 1 - c, stage(0, 1 - c), r0, nr, nc)
        d0_copy(p, c).start()
        place(e, xd.at[c, 0], r0, nr, nc)

    other = (1 - dp, e, t)

    def z_copy(u, k, r0, nr, f):
        r = pl.ds(r0, nr)
        return at(zs.at[k % 2, f, :, r], zr.at[k, f, :, r], z_ss.at[u, f], z_rs.at[u, f], other)

    def x_copy(m, p):
        if p == 0:
            return pltpu.make_async_copy(xd.at[m, 3], xd_hbm.at[m, pl.ds(0, RC)], x_sem.at[m, p])
        return pltpu.make_async_copy(
            xd.at[m, 0, pl.ds(*LATE)], xd_hbm.at[m, pl.ds(RC, LATE[1])], x_sem.at[m, p]
        )

    def z_left(u):
        k, part = UNITS[u]
        loop(0, NF, lambda f: z_copy(u, k, *part, f).wait_send())

    def project(u):
        k, (r0, nr) = UNITS[u]
        s = k % 2

        def piece(f):
            for m in range(2):
                v = jnp.dot(xd[m, k, r0 : r0 + nr], w[m, f], preferred_element_type=F32)
                own[s, f, m, r0 : r0 + nr] = v
                zs[s, f, m, r0 : r0 + nr] = v.astype(BF)
            z_copy(u, k, r0, nr, f).start()

        loop(0, NF, piece)

    first(0)
    for m in range(2):
        for f in range(NF):
            w_copy(m, f).wait()
    d0_copy(0, 1 - c).wait_recv()
    project(0)
    first(1)
    d0_copy(1, 1 - c).wait_recv()
    project(1)

    def dispatch(i):
        k, c2 = i // 2, i % 2
        place(((y + 4 - away(k)) % 4) * 2 + c2, stage(k, c2), 0, RC, TOKC)
        d_copy(k, c2).start()

    loop(2, 8, dispatch)
    cols = pl.ds(pl.multiple_of(c * 2 * GRP, 2 * GRP), 2 * GRP)
    rio = lax.broadcasted_iota(jnp.int32, (8, PR, 2 * GRP), 1) + c * (2 * CAP)
    hot = jnp.where(rio.astype(F32) == slotcol[:, :, cols], 1.0, 0.0).reshape(8 * PR, 2 * GRP)
    unhot[...] = hot.T.astype(BF)

    def ad_copy(m, p, f):
        cols = pl.ds(pl.multiple_of(f * fc, fc), fc)
        if p == 0:
            src, dst = ad.at[3, m, :, cols], ad_hbm.at[m, pl.ds(0, RC), cols]
        else:
            src, dst = ad.at[0, m, pl.ds(*LATE), cols], ad_hbm.at[m, pl.ds(RC, LATE[1]), cols]
        return pltpu.make_async_copy(src, dst, o_sem.at[m, p, f])

    def c1_copy(v, k, r0, nr, j):
        xb = (x + j) % 4
        r = pl.ds(r0, nr)
        return at(
            c1s.at[xb, r], c1r.at[v % 2, x, r], c1_ss.at[v, j], c1_rs.at[v, x], (dp, e, zlo * 4 + xb)
        )

    def c2_copy(k, c2):
        dev = (dp, ((y + AWAY[k]) % 4) * 2 + c2, t)
        return at(c2s.at[k, c2], res.at[e], c2_ss.at[k, c2], c2_rs.at[e], dev)

    def g_copy(m, i):
        dst = gu_hbm if m == 0 else gd_hbm
        rows = pl.ds(pl.multiple_of((i // NG) * xb_w, xb_w), xb_w)
        cols = pl.ds(pl.multiple_of((i % NG) * gc, gc), gc)
        return pltpu.make_async_copy(gs.at[i % 2], dst.at[rows, cols], g_sem.at[m, i % 2])

    def gradients(m, lo, hi):
        def band(n):
            rows = pl.ds(pl.multiple_of(n * xb_w, xb_w), xb_w)
            turned[...] = xd[m, 0:3, :, rows].reshape(3 * RC, xb_w).T
            turned[:, LATE[0] : RC] = jnp.zeros((xb_w, LATE[1]), BF)

            def tile(f):
                i = n * NG + f

                @pl.when(i >= 2)
                def _():
                    g_copy(m, i - 2).wait()

                if m == 1:

                    @pl.when(i < 2)
                    def _():
                        g_copy(0, i + 4 * NG - 2).wait()

                cols = pl.ds(pl.multiple_of(f * gc, gc), gc)
                right = ad[0:3, 1 - m, :, cols].reshape(3 * RC, gc)
                v = jnp.dot(turned[...], right, preferred_element_type=F32)
                gs[i % 2] = v.astype(BF)
                g_copy(m, i).start()

            loop(0, NG, tile)

        loop(lo, hi, band)

    def absorb(u):
        k, (r0, nr) = UNITS[u]
        s = k % 2
        r = slice(r0, r0 + nr)
        ar = slice(RC, RC + nr) if u == 5 else r
        acc[:, ar] = jnp.zeros((4, nr, xb_w), F32)

        def piece(f):
            z_copy(u, k, r0, nr, f).wait_recv()
            up = own[s, f, 0, r] + zr[k, f, 0, r].astype(F32)
            da = own[s, f, 1, r] + zr[k, f, 1, r].astype(F32)
            sg = jax.nn.sigmoid(up)
            cols = pl.ds(pl.multiple_of(f * fc, fc), fc)
            ad[k, 0, r, cols] = (up * sg).astype(BF)
            du = (da * sg * (1.0 + up * (1.0 - sg))).astype(BF)
            ad[k, 1, r, cols] = du
            if u >= 4:
                ad_copy(0, u - 4, f).start()
                ad_copy(1, u - 4, f).start()
            for n in range(4):
                acc[n, ar] += lax.dot_general(
                    du,
                    w[0, f, n * xb_w : (n + 1) * xb_w, :],
                    (((1,), (1,)), ((), ())),
                    preferred_element_type=F32,
                )

        loop(0, NF, piece)

    def c1_left(v):
        k, part = SUMS[v]
        loop(1, 4, lambda j: c1_copy(v, k, *part, j).wait_send())

    def spread(v):
        k, (r0, nr) = SUMS[v]
        if 0 < v < 4:
            c1_left(v - 1)

        def send(j):
            xb = (x + j) % 4
            c1s[xb, r0 : r0 + nr] = acc[xb, r0 : r0 + nr].astype(BF)
            c1_copy(v, k, r0, nr, j).start()

        loop(1, 4, send)

    def collect(v):
        k, (r0, nr) = SUMS[v]
        total = acc[x, r0 : r0 + nr]
        for j in range(1, 4):
            xs = (x + j) % 4
            r = c1r.at[v % 2, xs, pl.ds(r0, nr)]
            at(r, r, c1_ss.at[0, 0], c1_rs.at[v, xs], other).wait_recv()
            total += c1r[v % 2, xs, r0 : r0 + nr].astype(F32)
        return total

    def give_back(k, c2, part):
        part = jnp.concatenate([part, jnp.zeros((PR - 2 * CAP, xb_w), F32)], axis=0).astype(BF)
        if k > 0:
            c2s[k, c2] = part
            c2_copy(k, c2).start()
        else:

            @pl.when(c == c2)
            def _():
                res[e] = part

            @pl.when(c != c2)
            def _():
                c2s[k, c2] = part
                c2_copy(k, c2).start()

    for k in range(4):
        if k < 3:
            d_wait(0, k + 1)
            d_wait(1, k + 1)
            if k == 1:
                z_left(0)
                z_left(1)
            if k == 2:
                z_left(2)
            project(k + 2)
        else:
            for m in range(2):
                for p in range(2):
                    x_copy(m, p).start()
            z_left(3)
            project(5)
        if k == 0:
            d0_copy(0, c).wait_send()
            d0_copy(1, c).wait_send()
            absorb(0)
            absorb(1)
        else:
            d_copy(k, 0).wait_send()
            d_copy(k, 1).wait_send()
            absorb(k + 1)
        spread(k)
        if k == 2:
            ad[0, :, LATE[0] :] = jnp.zeros((2, LATE[1], NF * fc), BF)
            gradients(0, 0, 4)
            gradients(1, 0, 1)
        if k == 3:
            absorb(5)
            spread(4)
        total = collect(k)
        give_back(k, 0, total[0 : 2 * CAP])
        if k == 0:
            held[...] = total[2 * CAP :]
        else:
            give_back(k, 1, total[2 * CAP :])

    gradients(1, 1, 2)
    give_back(0, 1, jnp.concatenate([held[...], collect(4)], axis=0))
    gradients(1, 2, 3)

    def res_wait(j):
        i = (e + j) % 8
        at(res.at[i], res.at[i], c2_ss.at[0, 0], c2_rs.at[i], other).wait_recv()

    loop(1, 8, res_wait)
    back = res[...].reshape(8 * PR, xb_w)
    fin_s[...] = jnp.dot(unhot[...], back, preferred_element_type=F32).astype(BF)

    spot = (dp * 4 + x) * 2 + zlo

    def f_copy(j):
        i = (me16 + j) % 16
        row = pl.multiple_of(i * 16, 16)
        return at(fin_s.at[pl.ds(row, 16), :], fin_r.at[spot], f_ss.at[j], f_rs.at[spot], (i // 8, e, i % 8))

    loop(1, 16, lambda j: f_copy(j).start())
    fin_r[spot] = fin_s[pl.ds(pl.multiple_of(me16 * 16, 16), 16), :]

    gradients(1, 3, 4)

    def f_wait(j):
        i = (spot + j) % 16
        at(fin_r.at[i], fin_r.at[i], f_ss.at[0], f_rs.at[i], other).wait_recv()

    loop(1, 16, f_wait)
    for b in range(8):
        v = fin_r[b * 2].astype(F32) + fin_r[b * 2 + 1].astype(F32)
        out[:, b * xb_w : (b + 1) * xb_w] = v.astype(BF)

    for j in range(3):
        met_copy(j).wait_send()
    tok_copy(1).wait_send()
    loop(1, 4, lambda j: cot_copy(j).wait_send())

    @pl.when(c == 1)
    def _():
        tok_copy(0).wait_send()
        loop(0, 24, lambda i: fwd_copy(i // 3, 1 + i % 3).wait_send())

    @pl.when(c == 0)
    def _():
        cot_copy(0).wait_send()


    z_left(4)
    z_left(5)
    c1_left(3)
    c1_left(4)
    c2_copy(0, 1 - c).wait_send()
    for k in range(1, 4):
        for c2 in range(2):
            c2_copy(k, c2).wait_send()
    loop(1, 16, lambda j: f_copy(j).wait_send())
    for m in range(2):
        for f in range(NF):
            ad_copy(m, 0, f).wait()
            ad_copy(m, 1, f).wait()
        x_copy(m, 0).wait()
        x_copy(m, 1).wait()
    g_copy(1, 4 * NG - 2).wait()
    g_copy(1, 4 * NG - 1).wait()


def finish(up_part, down_part, xd, ad, gu, gd):
    for m, (part, dst) in enumerate(((up_part, gu), (down_part, gd))):
        last = lax.dot_general(
            xd[m], ad[1 - m], (((0,), (0,)), ((), ())), preferred_element_type=F32
        )
        dst[...] = (part[...].astype(F32) + last).astype(BF)


def shards(tokens, cotangent, expert_ids, route_weight, w_up, w_down):
    half, ff = w_up.shape[1], w_up.shape[2]
    rows = 4 * RC
    fc = ff // NF
    xb_w = half // 4
    vmem = pl.BlockSpec(memory_space=pltpu.VMEM)
    hbm = pl.BlockSpec(memory_space=pl.ANY)
    dma = pltpu.SemaphoreType.DMA
    grad = jax.ShapeDtypeStruct((half, ff), BF)
    out, xd, ad, gu, gd = pl.pallas_call(
        kernel,
        out_shape=(
            jax.ShapeDtypeStruct(cotangent.shape, BF),
            jax.ShapeDtypeStruct((2, FIN, half), BF),
            jax.ShapeDtypeStruct((2, FIN, ff), BF),
            grad,
            grad,
        ),
        in_specs=[vmem] * 4 + [hbm] * 2,
        out_specs=(vmem, hbm, hbm, hbm, hbm),
        scratch_shapes=[
            pltpu.VMEM((2, NF, half, fc), BF),
            pltpu.VMEM((TOKC, half), BF),
            pltpu.VMEM((4, 4, GRP), F32),
            pltpu.VMEM((8, 1, TOKC), F32),
            pltpu.VMEM((8, 1, TOKC), F32),
            pltpu.VMEM((2, 4, RC, half), BF),
            pltpu.VMEM((2, NF, 2, RC, fc), F32),
            pltpu.VMEM((2, NF, 2, RC, fc), BF),
            pltpu.VMEM((4, NF, 2, RC, fc), BF),
            pltpu.VMEM((4, 2, RC, ff), BF),
            pltpu.VMEM((4, FIN, xb_w), F32),
            pltpu.VMEM((4, FIN, xb_w), BF),
            pltpu.VMEM((2, 4, FIN, xb_w), BF),
            pltpu.VMEM((4, 2, PR, xb_w), BF),
            pltpu.VMEM((8, PR, xb_w), BF),
            pltpu.VMEM((2 * GRP, xb_w), BF),
            pltpu.VMEM((16, 16, xb_w), BF),
            pltpu.VMEM((2 * GRP, 8 * PR), BF),
            pltpu.VMEM((EARLY[1] - 2 * CAP, xb_w), F32),
            pltpu.VMEM((xb_w, 3 * RC), BF),
            pltpu.VMEM((2, xb_w, ff // NG), BF),
            dma((2, NF)),
            dma((4,)),
            dma((8, 3)),
            dma((32,)),
            dma((2,)),
            dma((4,)),
            dma((3,)),
            dma((4,)),
            dma((2,)),
            dma((2,)),
            dma((4, 2)),
            dma((2, 4)),
            dma((6, NF)),
            dma((6, NF)),
            dma((5, 4)),
            dma((5, 4)),
            dma((4, 2)),
            dma((8,)),
            dma((16,)),
            dma((16,)),
            dma((2, 2, NF)),
            dma((2, 2)),
            dma((2, 2)),
        ],
        compiler_params=pltpu.CompilerParams(
            collective_id=0, has_side_effects=True, vmem_limit_bytes=int(38.75 * 2**20)
        ),
        cost_estimate=pl.CostEstimate(
            flops=6 * rows * half * ff, bytes_accessed=4 * half * ff, transcendentals=rows * ff
        ),
    )(tokens, cotangent, expert_ids.T, route_weight.T, w_up, w_down)

    gb = 512
    gu, gd = pl.pallas_call(
        finish,
        grid=(half // gb,),
        out_shape=(grad, grad),
        in_specs=[
            pl.BlockSpec((gb, ff), lambda i: (i, 0)),
            pl.BlockSpec((gb, ff), lambda i: (i, 0)),
            pl.BlockSpec((2, FIN, gb), lambda i: (0, 0, i)),
            pl.BlockSpec((2, FIN, ff), lambda i: (0, 0, 0)),
        ],
        out_specs=(pl.BlockSpec((gb, ff), lambda i: (i, 0)),) * 2,
        compiler_params=pltpu.CompilerParams(vmem_limit_bytes=24 * 2**20),
    )(gu, gd, xd, ad)
    return out, gu[None], gd[None]


def solution(mesh):
    placed = (
        P(("dp", "expert"), None),
        P(("dp", "expert", "tensor"), None),
        P(("dp", "expert"), None),
        P(("dp", "expert"), None),
        P("expert", "dp", "tensor"),
        P("expert", "dp", "tensor"),
    )
    return jax.shard_map(
        shards,
        mesh=mesh,
        in_specs=placed,
        out_specs=(
            P(("dp", "expert", "tensor"), None),
            P("expert", "dp", "tensor"),
            P("expert", "dp", "tensor"),
        ),
        check_vma=False,
    )
```
